256 devices in a mesh: seq: 64 (over z, x, core), head: 4 (over y).
Axes of the slice: x: 4, y: 4, z: 8, core: 2. Of those that a mesh axis runs over, the one named last changes fastest.
Arguments:
- queries: bfloat16 [32768, 4096], P('seq', 'head'), may hold values from -200 to 200
- key_rows: bfloat16 [32768, 1024], P('seq', 'head'), may hold values from -6 to 6
- value_rows: bfloat16 [32768, 1024], P('seq', 'head'), may hold values from -6 to 6
- doc_lengths: int32 [64], replicated, may hold values from 1 to 3584, as said below
- block_plan: int32 [256], P('seq'), may hold values from 0 to 255, as said below
- out_weight: bfloat16 [4096, 4096], P('head'), may hold values from -0.125 to 0.125
Outputs:
- projected: bfloat16 [32768, 4096], P('seq', 'head')
The draws below stay inside these ranges and needn't reach their ends.
Inputs may be any that keep to these rules, and one draw needn't show every extreme that they name: `doc_lengths`: the lengths sum to 32768; the largest is exactly 3584. `block_plan`: every block number occurs once. The 4 entries of index i of seq hold first 2 blocks of index i itself in increasing order, then, in increasing order, the blocks of index i XOR 32 that are not among that index's own first 2 entries.
All inputs are finite; a program needn't handle non-finite values.
Results may differ from the reference program's by a relative error of at most 0.014.
Values may be sent and summed in bfloat16 or wider, within the bound.
A program may use at most 128 MiB of HBM per device.

```python
import jax
import jax.numpy as jnp
import numpy as np
from jax import lax

D = 4096
Q_HEADS = 32
KV_HEADS = 8
HEAD_DIM = 128
BLOCKS_DEV = 4
KEPT = 2
BLOCK = 128
SEQ_LEN = 32768
NBLOCKS = 256
MAX_DOC = 3584
DOCS = 64
GROUPS = 4


SUBSETS = np.array([[1, 1, 0, 0], [1, 0, 1, 0], [1, 0, 0, 1], [0, 1, 1, 0], [0, 1, 0, 1], [0, 0, 1, 1]], np.int32)


def documents(key):
    weight_key = jax.random.fold_in(key, 101)
    spot_key = jax.random.fold_in(key, 102)
    weights = jax.random.randint(weight_key, (DOCS - 1,), 500, 1500).astype(jnp.int32)
    spare_tokens = SEQ_LEN - MAX_DOC
    floor_share = spare_tokens * weights // jnp.sum(weights)
    leftover = spare_tokens - jnp.sum(floor_share)
    others = floor_share + (jnp.arange(DOCS - 1, dtype=jnp.int32) < leftover).astype(jnp.int32)
    long_spot = jax.random.randint(spot_key, (), 0, DOCS).astype(jnp.int32)
    doc_index = jnp.arange(DOCS, dtype=jnp.int32)
    source = jnp.clip(doc_index - (doc_index > long_spot).astype(jnp.int32), 0, DOCS - 2)
    return jnp.where(doc_index == long_spot, MAX_DOC, others[source]).astype(jnp.int32)


def alignment(key):
    key_base = jax.random.normal(jax.random.fold_in(key, 201), (SEQ_LEN, KV_HEADS, HEAD_DIM), jnp.float32)
    key_base = jnp.clip(key_base, -6.0, 6.0)
    return key_base


def draw_doc_lengths(key, part):
    lengths = documents(key)
    return lengths


def draw_block_plan(key, part):
    lengths = documents(key)
    doc_ends = jnp.cumsum(lengths).astype(jnp.int32)
    doc_begins = doc_ends - lengths
    positions = jnp.arange(SEQ_LEN, dtype=jnp.int32)
    starts = jnp.max(jnp.where(doc_begins[None, :] <= positions[:, None], doc_begins[None, :], 0), axis=1)
    devices = NBLOCKS // BLOCKS_DEV
    half_count = devices // 2
    block_load = (positions - starts + 1).reshape(NBLOCKS, BLOCK).sum(axis=1).reshape(devices, BLOCKS_DEV)
    subset_mask = jnp.asarray(SUBSETS, jnp.int32)
    signed = 2 * subset_mask - 1
    lead_gap = jnp.sum(block_load[:half_count, None, :] * signed[None], axis=2)
    trail_gap = jnp.sum(block_load[half_count:, None, :] * signed[None], axis=2)
    imbalance = jnp.abs(lead_gap[:, :, None] - trail_gap[:, None, :]).reshape(half_count, 36)
    ranking = imbalance * 36 + jnp.arange(36, dtype=jnp.int32)[None, :]
    chosen = jnp.argsort(ranking, axis=1, stable=True)[:, 0].astype(jnp.int32)
    mask_low = subset_mask[chosen // 6]
    mask_high = subset_mask[chosen % 6]
    order_low = jnp.argsort(1 - mask_low, axis=1, stable=True).astype(jnp.int32)
    order_high = jnp.argsort(1 - mask_high, axis=1, stable=True).astype(jnp.int32)
    low_devices = jnp.arange(half_count, dtype=jnp.int32)
    low_ids = low_devices[:, None] * BLOCKS_DEV + order_low
    high_ids = (low_devices[:, None] + half_count) * BLOCKS_DEV + order_high
    plan_low = jnp.concatenate([low_ids[:, :KEPT], high_ids[:, KEPT:]], axis=1)
    plan_high = jnp.concatenate([high_ids[:, :KEPT], low_ids[:, KEPT:]], axis=1)
    return jnp.concatenate([plan_low, plan_high], axis=0).reshape(NBLOCKS).astype(jnp.int32)


def draw_queries(key, part):
    key = jax.random.fold_in(key, 3)
    drawn_rows = jnp.clip(jax.random.normal(key, (SEQ_LEN, Q_HEADS, HEAD_DIM), jnp.float32), -6.0, 6.0)
    return drawn_rows.reshape(SEQ_LEN, Q_HEADS * HEAD_DIM).astype(jnp.bfloat16)


def draw_key_rows(key, part):
    key_base = alignment(key)
    return key_base.reshape(SEQ_LEN, KV_HEADS * HEAD_DIM).astype(jnp.bfloat16)


def raised(values, stream_key, source, target, blocks, factor):
    def block_of(dim):
        return (jnp.arange(values.shape[dim]) // (values.shape[dim] // blocks)).reshape((-1,) + (1,) * (values.ndim - 1 - dim))

    one_side = jax.random.permutation(stream_key, blocks)[block_of(target)]
    second = (block_of(target) + blocks // 2) % blocks
    return jnp.where((block_of(source) == one_side) | (block_of(source) == second), factor * values, values)


def steps_of(own_key, extent, cuts, low, top_value):
    gain = 1.0
    for axis_at, shards_of in cuts:
        steps = jax.random.uniform(jax.random.fold_in(jax.random.fold_in(own_key, 6), axis_at), (shards_of,), jnp.float32, low / len(cuts), top_value / len(cuts))
        gain = gain * jnp.repeat(jnp.exp(steps), extent[axis_at] // shards_of).reshape((-1,) + (1,) * (len(extent) - 1 - axis_at))
    return gain


def noise(key, dims, scale, limit, split=(), kind=jnp.bfloat16):
    drawn = jax.random.normal(key, dims, jnp.float32) * scale
    if len(split) > 0:
        drawn = steps_of(key, dims, split, -0.22, 0.18) * drawn
    return jnp.clip(drawn, min=-limit, max=limit).astype(kind)


def bell_draw_with(rng, shape, spread, most, pieces, heavy, held_as=jnp.bfloat16):
    result = spread * jax.random.normal(rng, shape, jnp.float32)
    if pieces:
        result = result * steps_of(rng, shape, pieces, -0.22, 0.18)
    return jnp.clip(raised(result, jax.random.fold_in(rng, 3), *heavy), -most, most).astype(held_as)


def setup_inputs(seed: int = 0) -> dict:
    arg_keys = jax.random.split(jax.random.key(seed), 7)
    queries = draw_queries(jax.random.fold_in(arg_keys[6], 71), 0)
    key_rows = draw_key_rows(jax.random.fold_in(arg_keys[6], 71), 0)
    value_rows = noise(arg_keys[2], (SEQ_LEN, KV_HEADS * HEAD_DIM), 1.0, 6.0, ((0, 64), (1, 4)))
    doc_lengths = draw_doc_lengths(jax.random.fold_in(arg_keys[6], 71), 0)
    block_plan = draw_block_plan(jax.random.fold_in(arg_keys[6], 71), 0)
    out_weight = bell_draw_with(arg_keys[5], (Q_HEADS * HEAD_DIM, D), (Q_HEADS * HEAD_DIM) ** -0.5, 0.125, ((0, 4),), (0, 1, 4, 2.0))
    return {"queries": queries, "key_rows": key_rows, "value_rows": value_rows, "doc_lengths": doc_lengths, "block_plan": block_plan, "out_weight": out_weight}


NEG = -1.0e30


def doc_starts(doc_lengths, positions):
    doc_ends = jnp.cumsum(doc_lengths).astype(jnp.int32)
    doc_begins = doc_ends - doc_lengths
    inside = doc_begins[None, :] <= positions[:, None]
    return jnp.max(jnp.where(inside, doc_begins[None, :], 0), axis=1).astype(jnp.int32)


def reference(queries, key_rows, value_rows, doc_lengths, block_plan, out_weight):
    total_len = queries.shape[0]
    group_size = Q_HEADS // KV_HEADS
    positions = jnp.arange(total_len, dtype=jnp.int32)
    starts = doc_starts(doc_lengths, positions)
    pad_keys = jnp.concatenate([jnp.zeros((MAX_DOC, key_rows.shape[1]), key_rows.dtype), key_rows], 0)
    pad_values = jnp.concatenate([jnp.zeros((MAX_DOC, value_rows.shape[1]), value_rows.dtype), value_rows], 0)
    score_scale = HEAD_DIM ** -0.5

    def one_block(block_id):
        first = (block_id * BLOCK).astype(jnp.int32)
        query_block = lax.dynamic_slice_in_dim(queries, first, BLOCK, 0).astype(jnp.float32)
        query_block = query_block.reshape(BLOCK, KV_HEADS, group_size, HEAD_DIM)
        query_pos = first + jnp.arange(BLOCK, dtype=jnp.int32)
        query_start = lax.dynamic_slice_in_dim(starts, first, BLOCK, 0)
        key_tile = lax.dynamic_slice_in_dim(pad_keys, first, MAX_DOC + BLOCK, 0).astype(jnp.float32)
        key_tile = key_tile.reshape(MAX_DOC + BLOCK, KV_HEADS, HEAD_DIM)
        value_tile = lax.dynamic_slice_in_dim(pad_values, first, MAX_DOC + BLOCK, 0).astype(jnp.float32)
        value_tile = value_tile.reshape(MAX_DOC + BLOCK, KV_HEADS, HEAD_DIM)
        key_pos = first - MAX_DOC + jnp.arange(MAX_DOC + BLOCK, dtype=jnp.int32)
        scores = jnp.einsum("tgrd,ugd->grtu", query_block, key_tile) * score_scale
        allowed = jnp.logical_and(key_pos[None, :] >= query_start[:, None], key_pos[None, :] <= query_pos[:, None])
        masked = jnp.where(allowed, scores, NEG)
        row_max = jnp.max(masked, axis=3)
        weights = jnp.where(allowed, jnp.exp(masked - row_max[..., None]), 0.0)
        rounded = lax.optimization_barrier(weights.astype(jnp.bfloat16)).astype(jnp.float32)
        mixed = jnp.einsum("grtu,ugd->grtd", rounded, value_tile)
        normed = mixed / jnp.sum(weights, axis=3)[..., None]
        normed = jnp.transpose(normed, (2, 0, 1, 3)).reshape(BLOCK, Q_HEADS * HEAD_DIM)
        return normed.astype(jnp.bfloat16)

    heads_out = lax.map(one_block, block_plan).reshape(total_len, Q_HEADS * HEAD_DIM)
    per_group = Q_HEADS * HEAD_DIM // GROUPS

    def add_group(group_index, summed):
        offset = (group_index * per_group)
        columns = lax.dynamic_slice_in_dim(heads_out, offset, per_group, 1)
        weight_rows = lax.dynamic_slice_in_dim(out_weight, offset, per_group, 0)
        partial_value = jnp.dot(columns, weight_rows, preferred_element_type=jnp.float32)
        partial_value = lax.optimization_barrier(partial_value.astype(jnp.bfloat16)).astype(jnp.float32)
        return summed + partial_value

    summed = lax.fori_loop(0, GROUPS, add_group, jnp.zeros((total_len, D), jnp.float32))
    return summed.astype(jnp.bfloat16)
```

```python
import jax
import jax.numpy as jnp
from jax import lax
from jax.experimental import pallas as pl
from jax.experimental.pallas import tpu as pltpu
from jax.sharding import PartitionSpec as P

MESH = pl.DeviceIdType.MESH
F32 = jnp.float32
BF16 = jnp.bfloat16
HEAD_DIM = 128
DOCS = 64
X_CHIPS = 4
Z_CHIPS = 8
CHIPS = X_CHIPS * Z_CHIPS
HEADS = 8
KV = 2
T = 512
BLOCK = 128
WIDE = 1024
HALF = 512
VROWS = HEAD_DIM + 16
EXP_SCALE = 1.4426950408889634 / HEAD_DIM**0.5
BIG = 1e30
OWN, CROSS, NEAR, NEAR_O, FAR, FAR_O, MID, MID_O, ABOVE = range(9)
DUMMY = 8


def transposed(block):
    return block.astype(F32).T.astype(BF16)


def kernel(
    q_hbm, k_hbm, v_hbm, lens, plan, w_hbm, out,
    qv, win, relay, wbuf, ka, vat, qt, m_ref, acc, s0, s1, p0, p1, a0, a1,
    att, keep, sent, landed, res, moved_in,
    in_sem, w_sem, kv_send, kv_recv, y_send, y_recv, z_send, z_recv,
):
    index = lax.axis_index("seq")
    y = lax.axis_index("head")
    core = lax.rem(index, 2)
    chip = index // 2
    x = lax.rem(chip, X_CHIPS)
    z = chip // X_CHIPS

    def at(zz, xx, cc):
        return ((zz * X_CHIPS + xx) * 2 + cc, y)

    z_up = at(lax.rem(z + 1, Z_CHIPS), x, core)
    z_down = at(lax.rem(z + Z_CHIPS - 1, Z_CHIPS), x, core)
    x_up = at(z, lax.rem(x + 1, X_CHIPS), core)
    x_down = at(z, lax.rem(x + X_CHIPS - 1, X_CHIPS), core)
    sibling = at(z, x, 1 - core)
    partner = at(lax.rem(z + Z_CHIPS // 2, Z_CHIPS), x, core)
    y_up = (index, lax.rem(y + 1, 4))
    y_down = (index, lax.rem(y + 3, 4))

    load_k = pltpu.make_async_copy(k_hbm, win.at[OWN, :, pl.ds(0, 256)], in_sem.at[0])
    load_v = pltpu.make_async_copy(v_hbm, win.at[OWN, :, pl.ds(256, 256)], in_sem.at[1])
    load_q = pltpu.make_async_copy(q_hbm, qv, in_sem.at[2])
    load_k.start()
    load_v.start()
    load_q.start()
    load_w = []
    for step in (2, 1, 3, 0):
        group = lax.rem(y + step, 4)
        load_w.append(
            pltpu.make_async_copy(
                w_hbm.at[:, pl.ds(pl.multiple_of(group * WIDE, WIDE), WIDE)], wbuf.at[step], w_sem.at[step]
            )
        )

    barrier = pltpu.get_barrier_semaphore()
    for other in (z_up, z_down, x_up, x_down, sibling, partner, y_up, y_down):
        pl.semaphore_signal(barrier, inc=1, device_id=other, device_id_type=MESH)
    pl.semaphore_wait(barrier, 8)

    def part(ref, half):
        return ref.at[pl.ds(half * 256, 256), :]

    def send(source, slot, half, target):
        return pltpu.make_async_remote_copy(
            src_ref=part(win.at[source], half),
            dst_ref=part(win.at[slot], half),
            send_sem=kv_send.at[slot, half],
            recv_sem=kv_recv.at[slot, half],
            device_id=target,
            device_id_type=MESH,
        )

    def send_relay(source, half, way, target):
        return pltpu.make_async_remote_copy(
            src_ref=part(win.at[source], half),
            dst_ref=relay.at[way],
            send_sem=kv_send.at[9, way],
            recv_sem=kv_recv.at[9, way],
            device_id=target,
            device_id_type=MESH,
        )

    def pass_relay(half, way, target):
        return pltpu.make_async_remote_copy(
            src_ref=relay.at[way],
            dst_ref=part(win.at[MID], half),
            send_sem=kv_send.at[MID, half],
            recv_sem=kv_recv.at[MID, half],
            device_id=target,
            device_id_type=MESH,
        )

    load_k.wait()
    load_v.wait()

    for half in (0, 1):
        send(OWN, ABOVE, half, z_up).start()

        @pl.when(x < 3)
        def _():
            send(OWN, NEAR, half, x_up).start()

        @pl.when(x == 0)
        def _():
            send(OWN, FAR, half, x_down).start()

        @pl.when(core == 0)
        def _():
            send(OWN, CROSS, half, sibling).start()

    @pl.when(x == 1)
    def _():
        send_relay(OWN, 1, 1, x_down).start()

    for copy in load_w:
        copy.start()

    lane = lax.broadcasted_iota(jnp.int32, (1, HEAD_DIM), 1)
    begins = jnp.zeros((1, HEAD_DIM), jnp.int32)
    ends = jnp.zeros((1, HEAD_DIM), jnp.int32)
    for doc in range(DOCS):
        length = lens[doc]
        begins = begins + jnp.where(lane > doc, length, 0)
        ends = ends + jnp.where(lane >= doc, length, 0)
    kept0 = jnp.clip(plan[0] - index * 4, 0, 3)
    kept1 = jnp.clip(plan[1] - index * 4, 0, 3)
    moved0 = jnp.where(kept0 != 0, 0, jnp.where(kept1 != 1, 1, 2))
    moved1 = jnp.clip(6 - kept0 - kept1 - moved0, 0, 3)
    ids = (moved0, moved1, kept0, kept1)

    def same_doc(base, rows):
        pos = base + lax.broadcasted_iota(jnp.int32, (rows, HEAD_DIM), 0)
        return jnp.logical_and(pos >= begins, pos < ends)

    for g in range(2 * 8):
        vat[g, HEAD_DIM:, :] = jnp.ones((VROWS - HEAD_DIM, T), BF16)
    load_q.wait()
    for b in range(4):
        rows = qv[ids[b]]
        marks = jnp.where(same_doc(index * T + ids[b] * BLOCK, BLOCK), 0.0, -BIG).T.astype(BF16)
        for h in range(HEADS):
            c = (b // 2) * 4 + h // 2
            col = (h % 2) * 256 + (b % 2) * BLOCK
            qt[c, :HEAD_DIM, col : col + BLOCK] = transposed(rows[:, h * HEAD_DIM : (h + 1) * HEAD_DIM])
            qt[c, HEAD_DIM:, col : col + BLOCK] = marks
    m_ref[...] = jnp.full(m_ref.shape, -3e38, F32)
    acc[...] = jnp.zeros(acc.shape, F32)

    def prepare(tile, base):
        hot = jnp.where(same_doc(base, T), 1.0, 0.0).astype(BF16)
        for g in range(KV):
            ka[2 * tile + g, :, :HEAD_DIM] = win[tile, :, g * HEAD_DIM : (g + 1) * HEAD_DIM]
            ka[2 * tile + g, :, HEAD_DIM:] = hot
            vat[2 * tile + g, :HEAD_DIM, :] = transposed(win[tile, :, 256 + g * HEAD_DIM : 256 + (g + 1) * HEAD_DIM])

    scores, probs, scales = (s0, s1), (p0, p1), (a0, a1)

    def score(kg, c, which, causal):
        value = jnp.dot(ka[kg], qt[c], preferred_element_type=F32)
        if causal is not None:
            value = jnp.where(causal, value, -BIG)
        scores[which][...] = value

    def soften(c, which):
        value = scores[which][...]
        old = m_ref[c]
        new = jnp.maximum(old, jnp.max(value, axis=0, keepdims=True))
        probs[which][...] = jnp.exp2((value - new) * EXP_SCALE).astype(BF16)
        scales[which][...] = jnp.exp2((old - new) * EXP_SCALE)
        m_ref[c] = new

    def weigh(kg, c, which):
        acc[c] = acc[c] * scales[which][...] + jnp.dot(vat[kg], probs[which][...], preferred_element_type=F32)

    prepare(OWN, index * T)
    lanes = lax.broadcasted_iota(jnp.int32, (T, T), 1)
    key_row = lax.broadcasted_iota(jnp.int32, (T, T), 0)
    inner = lanes % BLOCK
    second = (lanes // BLOCK) % 2
    limits = [inner + BLOCK * jnp.where(second == 0, ids[2 * half], ids[2 * half + 1]) for half in (0, 1)]

    def own_half(half):
        causal = key_row <= limits[half]
        for u in range(4):
            score(u // 2, half * 4 + u, u % 2, causal)
            soften(half * 4 + u, u % 2)
            weigh(u // 2, half * 4 + u, u % 2)

    own_half(0)
    own_half(1)

    for half in (0, 1):
        send(OWN, ABOVE, half, z_up).wait_recv()

        @pl.when(x == 2)
        def _():
            if half == 0:
                send_relay(ABOVE, 0, 0, x_up).start()

        @pl.when(x > 0)
        def _():
            send(ABOVE, FAR, half, x_down).start()

        @pl.when(x == 3)
        def _():
            send(ABOVE, NEAR, half, x_up).start()

        @pl.when(core == 1)
        def _():
            send(ABOVE, CROSS, half, sibling).start()

    @pl.when(x == 0)
    def _():
        send_relay(OWN, 1, 1, x_down).wait_recv()
        pass_relay(1, 1, x_down).start()

    def near_came():
        for half in (0, 1):
            send(OWN, NEAR, half, x_up).wait_recv()
            send(NEAR, NEAR_O, half, sibling).start()
            if half == 0:

                @pl.when(x != 3)
                def _():
                    send(NEAR, MID, 0, x_up).start()

    @pl.when(x != 0)
    def _():
        near_came()

    def came(slot):
        for half in (0, 1):
            send(OWN, slot, half, sibling).wait_recv()

    def far_came():
        for half in (0, 1):
            send(OWN, FAR, half, x_down).wait_recv()
            send(FAR, FAR_O, half, sibling).start()
            if half == 1:

                @pl.when(x != 0)
                def _():
                    send(FAR, MID, 1, x_down).start()

    def mid_came():
        for half in (0, 1):
            send(OWN, MID, half, x_up).wait_recv()
            send(MID, MID_O, half, sibling).start()

    def copy_y(kind, block, way):
        return pltpu.make_async_remote_copy(
            src_ref=sent.at[kind, block, way],
            dst_ref=landed.at[kind, block, way],
            send_sem=y_send.at[kind, block, way],
            recv_sem=y_recv.at[kind, block, way],
            device_id=y_up if way == 0 else y_down,
            device_id_type=MESH,
        )

    def give(kind, block, way, value):
        sent[kind, block, way] = value.astype(BF16)
        copy_y(kind, block, way).start()

    def project(block, step, part_index):
        return jnp.dot(
            att[block], wbuf[step, :, part_index * HALF : (part_index + 1) * HALF], preferred_element_type=F32
        )

    def first_step(block):
        for way in (0, 1):
            give(0, block, way, project(block, 2, way))
        give(1, block, 0, project(block, 1, 1))
        give(1, block, 1, project(block, 3, 0))
        keep[block, 0] = project(block, 1, 0)
        keep[block, 1] = project(block, 3, 1)

    def second_step(block):
        for way in (0, 1):
            copy_y(0, block, way).wait_recv()
            give(2, block, way, keep[block, way] + landed[0, block, way].astype(F32))

    def last_step(block):
        own = [project(block, 0, 0), project(block, 0, 1)]
        for kind, way in ((1, 0), (1, 1), (2, 0), (2, 1)):
            copy_y(kind, block, way).wait_recv()
        left = own[0] + landed[2, block, 0].astype(F32) + landed[1, block, 1].astype(F32)
        right = own[1] + landed[1, block, 0].astype(F32) + landed[2, block, 1].astype(F32)
        return left.astype(BF16), right.astype(BF16)

    def copy_z(block):
        return pltpu.make_async_remote_copy(
            src_ref=res.at[block],
            dst_ref=moved_in.at[block],
            send_sem=z_send.at[block],
            recv_sem=z_recv.at[block],
            device_id=partner,
            device_id_type=MESH,
        )

    def finish_moved(block):
        left, right = last_step(block)
        res[block, :, :HALF] = left
        res[block, :, HALF:] = right
        copy_z(block).start()

    def finish_kept(block):
        left, right = last_step(block)
        out[pl.ds((block - 2) * BLOCK, BLOCK), :HALF] = left
        out[pl.ds((block - 2) * BLOCK, BLOCK), HALF:] = right

    def normalise(half):
        for u in range(4):
            c = half * 4 + u
            value = acc[c]
            rows = (value[:HEAD_DIM] / value[HEAD_DIM : HEAD_DIM + 1]).T.astype(BF16)
            for r in range(2):
                h = u * 2 + r
                for b in range(2):
                    start = r * 256 + b * BLOCK
                    att[half * 2 + b, :, h * HEAD_DIM : (h + 1) * HEAD_DIM] = rows[start : start + BLOCK]

    back = (0, 1, 1, 3, 3, 2, 2)

    def run_half(half, hooks):
        def segment(s, carry):
            tile = s + 1
            for when, hook in hooks.items():
                pl.when(s == when)(hook)
            if half == 0:
                distance = jnp.where(tile >= MID, 2, jnp.where(tile >= FAR, 3, 1))
                side = jnp.where(lax.rem(tile, 2) == 0, core, 1 - core)
                distance = jnp.where(tile == CROSS, jnp.where(core == 0, 4, 0), distance)
                there = lax.rem(chip - distance + CHIPS, CHIPS)
                prepare(tile, (there * 2 + side) * T)
            first = s == 0
            for u in range(4):
                c = half * 4 + u
                score(2 * tile + u // 2, c, u % 2, None)
                soften(c - 1 if u else jnp.where(first, DUMMY, half * 4 + 3), (u + 1) % 2)
                if u >= 2:
                    weigh(2 * tile + (u - 2) // 2, c - 2, u % 2)
                else:
                    weigh(2 * s + 1, jnp.where(first, DUMMY, half * 4 + 2 + u), u % 2)
            return carry

        lax.fori_loop(0, 7, segment, 0)
        soften(half * 4 + 3, 1)
        weigh(15, half * 4 + 2, 0)
        weigh(15, half * 4 + 3, 1)

    def hook_near():
        pl.when(x == 0)(near_came)

    def hook_near_other():
        came(NEAR_O)

        @pl.when(x == 3)
        def _():
            send_relay(OWN, 0, 0, x_up).wait_recv()
            pass_relay(0, 0, x_up).start()

        far_came()

    run_half(
        0,
        {
            0: lambda: came(CROSS),
            1: hook_near,
            2: hook_near_other,
            4: lambda: came(FAR_O),
            5: mid_came,
            6: lambda: came(MID_O),
        },
    )
    normalise(0)
    for copy in load_w:
        copy.wait()
    first_step(0)
    first_step(1)
    run_half(
        1,
        {0: lambda: second_step(0), 2: lambda: second_step(1), 5: lambda: finish_moved(0)},
    )
    normalise(1)
    first_step(2)
    first_step(3)
    finish_moved(1)
    second_step(2)
    second_step(3)
    finish_kept(2)
    finish_kept(3)
    for block in (0, 1):
        copy_z(block).wait_recv()
        out[pl.ds((2 + block) * BLOCK, BLOCK), :] = moved_in[block]

    for half in (0, 1):
        for slot in (ABOVE, CROSS, NEAR, NEAR_O, FAR, FAR_O, MID, MID_O):
            send(OWN, slot, half, sibling).wait_send()

    @pl.when(x == 1)
    def _():
        send_relay(OWN, 1, 1, x_down).wait_send()

    @pl.when(x == 2)
    def _():
        send_relay(ABOVE, 0, 0, x_up).wait_send()

    for block in range(4):
        for kind in range(3):
            for way in (0, 1):
                copy_y(kind, block, way).wait_send()
    for block in (0, 1):
        copy_z(block).wait_send()


def local(queries, key_rows, value_rows, doc_lengths, block_plan, out_weight):
    tokens, width = queries.shape
    anywhere = pl.BlockSpec(memory_space=pl.ANY)
    scalars = pl.BlockSpec(memory_space=pltpu.SMEM)
    return pl.pallas_call(
        kernel,
        out_shape=jax.ShapeDtypeStruct((tokens, width), BF16),
        in_specs=[anywhere, anywhere, anywhere, scalars, scalars, anywhere],
        out_specs=pl.BlockSpec(memory_space=pltpu.VMEM),
        scratch_shapes=[
            pltpu.VMEM((4, BLOCK, width), BF16),
            pltpu.VMEM((9, T, 512), BF16),
            pltpu.VMEM((2, 256, 512), BF16),
            pltpu.VMEM((4, WIDE, WIDE), BF16),
            pltpu.VMEM((16, T, 256), BF16),
            pltpu.VMEM((16, VROWS, T), BF16),
            pltpu.VMEM((8, 256, T), BF16),
            pltpu.VMEM((9, 1, T), F32),
            pltpu.VMEM((9, VROWS, T), F32),
            pltpu.VMEM((T, T), F32),
            pltpu.VMEM((T, T), F32),
            pltpu.VMEM((T, T), BF16),
            pltpu.VMEM((T, T), BF16),
            pltpu.VMEM((1, T), F32),
            pltpu.VMEM((1, T), F32),
            pltpu.VMEM((4, BLOCK, WIDE), BF16),
            pltpu.VMEM((4, 2, BLOCK, HALF), F32),
            pltpu.VMEM((3, 4, 2, BLOCK, HALF), BF16),
            pltpu.VMEM((3, 4, 2, BLOCK, HALF), BF16),
            pltpu.VMEM((2, BLOCK, WIDE), BF16),
            pltpu.VMEM((2, BLOCK, WIDE), BF16),
            pltpu.SemaphoreType.DMA((3,)),
            pltpu.SemaphoreType.DMA((4,)),
            pltpu.SemaphoreType.DMA((10, 2)),
            pltpu.SemaphoreType.DMA((10, 2)),
            pltpu.SemaphoreType.DMA((3, 4, 2)),
            pltpu.SemaphoreType.DMA((3, 4, 2)),
            pltpu.SemaphoreType.DMA((2,)),
            pltpu.SemaphoreType.DMA((2,)),
        ],
        compiler_params=pltpu.CompilerParams(
            collective_id=0, has_side_effects=True, vmem_limit_bytes=56 << 20
        ),
        name="attend_and_project",
    )(queries.reshape(4, BLOCK, width), key_rows, value_rows, doc_lengths, block_plan, out_weight)


def solution(mesh):
    return jax.shard_map(
        local,
        mesh=mesh,
        in_specs=(
            P("seq", "head"),
            P("seq", "head"),
            P("seq", "head"),
            P(),
            P("seq"),
            P("head", None),
        ),
        out_specs=P("seq", "head"),
        check_vma=False,
    )
```

```python
import jax
import jax.numpy as jnp
from jax import lax
from jax.experimental import pallas as pl
from jax.experimental.pallas import tpu as pltpu
from jax.sharding import PartitionSpec as P

MESH = pl.DeviceIdType.MESH
F32 = jnp.float32
BF16 = jnp.bfloat16
HEAD_DIM = 128
DOCS = 64
X_CHIPS = 4
Z_CHIPS = 8
CHIPS = X_CHIPS * Z_CHIPS
HEADS = 8
KV = 2
T = 512
BLOCK = 128
QUARTER = 128
WIDE = 1024
HALF = 512
VROWS = HEAD_DIM + 16
EXP_SCALE = 1.4426950408889634 / HEAD_DIM**0.5
BIG = 1e30
OWN, CROSS, NEAR, NEAR_O, FAR, FAR_O, MID, MID_O, ABOVE = range(9)
DUMMY = 8


def transposed(block):
    return block.astype(F32).T.astype(BF16)


def kernel(
    q_hbm, k_hbm, v_hbm, lens, plan, w_hbm, out,
    qv, win, relay, wbuf, ka, vat, qt, m_ref, acc, s0, s1, p0, p1, a0, a1,
    att, keep, sent, landed, res, midway, moved_in,
    in_sem, w_sem, kv_send, kv_recv, y_send, y_recv, z_send, z_recv,
):
    index = lax.axis_index("seq")
    y = lax.axis_index("head")
    core = lax.rem(index, 2)
    chip = index // 2
    x = lax.rem(chip, X_CHIPS)
    z = chip // X_CHIPS

    def at(zz, xx, cc):
        return ((zz * X_CHIPS + xx) * 2 + cc, y)

    z_up = at(lax.rem(z + 1, Z_CHIPS), x, core)
    z_down = at(lax.rem(z + Z_CHIPS - 1, Z_CHIPS), x, core)
    x_up = at(z, lax.rem(x + 1, X_CHIPS), core)
    x_down = at(z, lax.rem(x + X_CHIPS - 1, X_CHIPS), core)
    sibling = at(z, x, 1 - core)
    way_z = jnp.where(core == 0, 2, Z_CHIPS - 2)
    onward = at(lax.rem(z + way_z, Z_CHIPS), x, core)
    behind = at(lax.rem(z + Z_CHIPS - way_z, Z_CHIPS), x, core)
    y_up = (index, lax.rem(y + 1, 4))
    y_down = (index, lax.rem(y + 3, 4))

    load_k = pltpu.make_async_copy(k_hbm, win.at[OWN, :, pl.ds(0, 256)], in_sem.at[0])
    load_v = pltpu.make_async_copy(v_hbm, win.at[OWN, :, pl.ds(256, 256)], in_sem.at[1])
    load_q = pltpu.make_async_copy(q_hbm, qv, in_sem.at[2])
    load_k.start()
    load_v.start()
    load_q.start()
    load_w = []
    for step in (2, 1, 3, 0):
        group = lax.rem(y + step, 4)
        load_w.append(
            pltpu.make_async_copy(
                w_hbm.at[:, pl.ds(pl.multiple_of(group * WIDE, WIDE), WIDE)], wbuf.at[step], w_sem.at[step]
            )
        )

    barrier = pltpu.get_barrier_semaphore()
    for other in (z_up, z_down, x_up, x_down, sibling, onward, behind, y_up, y_down):
        pl.semaphore_signal(barrier, inc=1, device_id=other, device_id_type=MESH)
    pl.semaphore_wait(barrier, 9)

    def part(ref, q):
        return ref.at[pl.ds(q * QUARTER, QUARTER), :]

    def send(source, slot, q, target):
        return pltpu.make_async_remote_copy(
            src_ref=part(win.at[source], q),
            dst_ref=part(win.at[slot], q),
            send_sem=kv_send.at[slot, q],
            recv_sem=kv_recv.at[slot, q],
            device_id=target,
            device_id_type=MESH,
        )

    def send_relay(source, q, target):
        return pltpu.make_async_remote_copy(
            src_ref=part(win.at[source], q),
            dst_ref=relay.at[q],
            send_sem=kv_send.at[9, q],
            recv_sem=kv_recv.at[9, q],
            device_id=target,
            device_id_type=MESH,
        )

    def hand_over(q, target):
        return pltpu.make_async_remote_copy(
            src_ref=relay.at[q],
            dst_ref=part(win.at[MID], q),
            send_sem=kv_send.at[10, q],
            recv_sem=kv_recv.at[MID, q],
            device_id=target,
            device_id_type=MESH,
        )

    def pass_relay(q, target):
        send_relay(OWN, q, target).wait_recv()
        hand_over(q, target).start()

    load_k.wait()
    load_v.wait()

    for q in range(4):
        send(OWN, ABOVE, q, z_up).start()

        @pl.when(x < 3)
        def _():
            send(OWN, NEAR, q, x_up).start()

        @pl.when(x == 0)
        def _():
            send(OWN, FAR, q, x_down).start()

        @pl.when(core == 0)
        def _():
            send(OWN, CROSS, q, sibling).start()

    for copy in load_w:
        copy.start()

    lane = lax.broadcasted_iota(jnp.int32, (1, HEAD_DIM), 1)
    begins = jnp.zeros((1, HEAD_DIM), jnp.int32)
    ends = jnp.zeros((1, HEAD_DIM), jnp.int32)
    for doc in range(DOCS):
        length = lens[doc]
        begins = begins + jnp.where(lane > doc, length, 0)
        ends = ends + jnp.where(lane >= doc, length, 0)
    kept0 = jnp.clip(plan[0] - index * 4, 0, 3)
    kept1 = jnp.clip(plan[1] - index * 4, 0, 3)
    moved0 = jnp.where(kept0 != 0, 0, jnp.where(kept1 != 1, 1, 2))
    moved1 = jnp.clip(6 - kept0 - kept1 - moved0, 0, 3)
    ids = (moved0, moved1, kept0, kept1)

    def same_doc(base, rows):
        pos = base + lax.broadcasted_iota(jnp.int32, (rows, HEAD_DIM), 0)
        return jnp.logical_and(pos >= begins, pos < ends)

    for g in range(2 * 8):
        vat[g, HEAD_DIM:, :] = jnp.ones((VROWS - HEAD_DIM, T), BF16)
    load_q.wait()
    for b in range(4):
        rows = qv[ids[b]]
        marks = jnp.where(same_doc(index * T + ids[b] * BLOCK, BLOCK), 0.0, -BIG).T.astype(BF16)
        for h in range(HEADS):
            c = (b // 2) * 4 + h // 2
            col = (h % 2) * 256 + (b % 2) * BLOCK
            qt[c, :HEAD_DIM, col : col + BLOCK] = transposed(rows[:, h * HEAD_DIM : (h + 1) * HEAD_DIM])
            qt[c, HEAD_DIM:, col : col + BLOCK] = marks
    m_ref[...] = jnp.full(m_ref.shape, -3e38, F32)
    acc[...] = jnp.zeros(acc.shape, F32)

    def prepare(tile, parts):
        for spot, (slot, start, base) in enumerate(parts):
            keys = pl.ds(spot * 256, 256)
            rows = pl.ds(start, 256)
            hot = jnp.where(same_doc(base, 256), 1.0, 0.0).astype(BF16)
            for g in range(KV):
                ka[2 * tile + g, keys, :HEAD_DIM] = win[slot, rows, g * HEAD_DIM : (g + 1) * HEAD_DIM]
                ka[2 * tile + g, keys, HEAD_DIM:] = hot
                vat[2 * tile + g, :HEAD_DIM, keys] = transposed(
                    win[slot, rows, 256 + g * HEAD_DIM : 256 + (g + 1) * HEAD_DIM]
                )

    scores, probs, scales = (s0, s1), (p0, p1), (a0, a1)

    def score(kg, c, which, causal):
        value = jnp.dot(ka[kg], qt[c], preferred_element_type=F32)
        if causal is not None:
            value = jnp.where(causal, value, -BIG)
        scores[which][...] = value

    def soften(c, which):
        value = scores[which][...]
        old = m_ref[c]
        new = jnp.maximum(old, jnp.max(value, axis=0, keepdims=True))
        probs[which][...] = jnp.exp2((value - new) * EXP_SCALE).astype(BF16)
        scales[which][...] = jnp.exp2((old - new) * EXP_SCALE)
        m_ref[c] = new

    def weigh(kg, c, which):
        acc[c] = acc[c] * scales[which][...] + jnp.dot(vat[kg], probs[which][...], preferred_element_type=F32)

    prepare(OWN, ((OWN, 0, index * T), (OWN, 256, index * T + 256)))
    lanes = lax.broadcasted_iota(jnp.int32, (T, T), 1)
    key_row = lax.broadcasted_iota(jnp.int32, (T, T), 0)
    inner = lanes % BLOCK
    second = (lanes // BLOCK) % 2
    limits = [inner + BLOCK * jnp.where(second == 0, ids[2 * half], ids[2 * half + 1]) for half in (0, 1)]

    def own_half(half):
        causal = key_row <= limits[half]
        for u in range(4):
            score(u // 2, half * 4 + u, u % 2, causal)
            soften(half * 4 + u, u % 2)
            weigh(u // 2, half * 4 + u, u % 2)

    def above_came(q):
        send(OWN, ABOVE, q, z_up).wait_recv()

        @pl.when(x > 0)
        def _():
            send(ABOVE, FAR, q, x_down).start()

        @pl.when(x == 3)
        def _():
            send(ABOVE, NEAR, q, x_up).start()

        @pl.when(core == 1)
        def _():
            send(ABOVE, CROSS, q, sibling).start()

    def near_came(q):
        send(OWN, NEAR, q, x_up).wait_recv()
        send(NEAR, NEAR_O, q, sibling).start()
        if q < 2:

            @pl.when(x != 3)
            def _():
                send(NEAR, MID, q, x_up).start()

            @pl.when(x == 3)
            def _():
                send_relay(NEAR, q, x_up).start()

    def far_came(q):
        send(OWN, FAR, q, x_down).wait_recv()
        send(FAR, FAR_O, q, sibling).start()
        if q >= 2:

            @pl.when(x != 0)
            def _():
                send(FAR, MID, q, x_down).start()

            @pl.when(x == 0)
            def _():
                send_relay(FAR, q, x_down).start()

    def mid_came(q):
        send(OWN, MID, q, x_up).wait_recv()
        send(MID, MID_O, q, sibling).start()

    def came(slot, *quarters):
        for q in quarters:
            send(OWN, slot, q, sibling).wait_recv()

    own_half(0)
    above_came(0)

    @pl.when(x != 0)
    def _():
        near_came(0)

    own_half(1)

    def copy_y(kind, block, way):
        return pltpu.make_async_remote_copy(
            src_ref=sent.at[kind, block, way],
            dst_ref=landed.at[kind, block, way],
            send_sem=y_send.at[kind, block, way],
            recv_sem=y_recv.at[kind, block, way],
            device_id=y_up if way == 0 else y_down,
            device_id_type=MESH,
        )

    def give(kind, block, way, value):
        sent[kind, block, way] = value.astype(BF16)
        copy_y(kind, block, way).start()

    def project(block, step, part_index):
        return jnp.dot(
            att[block], wbuf[step, :, part_index * HALF : (part_index + 1) * HALF], preferred_element_type=F32
        )

    def start_sum(block):
        for way in (0, 1):
            give(0, block, way, project(block, 2, way))

    def own_part(block):
        give(1, block, 0, project(block, 1, 1))
        give(1, block, 1, project(block, 3, 0))
        keep[block, 0] = project(block, 1, 0)
        keep[block, 1] = project(block, 3, 1)

    def second_step(block):
        for way in (0, 1):
            copy_y(0, block, way).wait_recv()
            give(2, block, way, keep[block, way] + landed[0, block, way].astype(F32))

    def last_step(block):
        own = [project(block, 0, 0), project(block, 0, 1)]
        for kind, way in ((1, 0), (1, 1), (2, 0), (2, 1)):
            copy_y(kind, block, way).wait_recv()
        left = own[0] + landed[2, block, 0].astype(F32) + landed[1, block, 1].astype(F32)
        right = own[1] + landed[1, block, 0].astype(F32) + landed[2, block, 1].astype(F32)
        return left.astype(BF16), right.astype(BF16)

    def copy_z(leg, block):
        return pltpu.make_async_remote_copy(
            src_ref=res.at[block] if leg == 0 else midway.at[block],
            dst_ref=midway.at[block] if leg == 0 else moved_in.at[block],
            send_sem=z_send.at[leg, block],
            recv_sem=z_recv.at[leg, block],
            device_id=onward,
            device_id_type=MESH,
        )

    def finish_moved(block):
        left, right = last_step(block)
        res[block, :, :HALF] = left
        res[block, :, HALF:] = right
        copy_z(0, block).start()

    def carry_moved(block):
        copy_z(0, block).wait_recv()
        copy_z(1, block).start()

    def finish_kept(block):
        left, right = last_step(block)
        out[pl.ds((block - 2) * BLOCK, BLOCK), :HALF] = left
        out[pl.ds((block - 2) * BLOCK, BLOCK), HALF:] = right

    def normalise(half):
        for u in range(4):
            c = half * 4 + u
            value = acc[c]
            rows = (value[:HEAD_DIM] / value[HEAD_DIM : HEAD_DIM + 1]).T.astype(BF16)
            for r in range(2):
                h = u * 2 + r
                for b in range(2):
                    start = r * 256 + b * BLOCK
                    att[half * 2 + b, :, h * HEAD_DIM : (h + 1) * HEAD_DIM] = rows[start : start + BLOCK]

    def run_half(half, hooks):
        def segment(s, carry):
            tile = s + 1
            for when, hook in hooks.items():
                pl.when(s == when)(hook)
            if half == 0:
                cross = tile == 3
                slot = jnp.where(cross, CROSS, jnp.where(tile >= 6, MID, jnp.where(lax.rem(tile, 3) == 1, NEAR, FAR)))
                distance = jnp.where(slot == MID, 2, jnp.where(slot == FAR, 3, 1))
                distance = jnp.where(cross, jnp.where(core == 0, 4, 0), distance)
                high = jnp.where(tile == 4, 1, jnp.where(tile == 5, 1, jnp.where(tile == 7, 1, 0)))
                there = 2 * lax.rem(chip - distance + CHIPS, CHIPS)
                start0 = pl.multiple_of(high * 256, 256)
                start1 = pl.multiple_of(jnp.where(cross, 256, high * 256), 256)
                slot1 = jnp.where(cross, CROSS, slot + 1)
                side0 = jnp.where(cross, 1 - core, core)
                prepare(
                    tile,
                    (
                        (slot, start0, (there + side0) * T + start0),
                        (slot1, start1, (there + 1 - core) * T + start1),
                    ),
                )
            first = s == 0
            for u in range(4):
                c = half * 4 + u
                score(2 * tile + u // 2, c, u % 2, None)
                soften(c - 1 if u else jnp.where(first, DUMMY, half * 4 + 3), (u + 1) % 2)
                if u >= 2:
                    weigh(2 * tile + (u - 2) // 2, c - 2, u % 2)
                else:
                    weigh(2 * s + 1, jnp.where(first, DUMMY, half * 4 + 2 + u), u % 2)
            return carry

        lax.fori_loop(0, 7, segment, 0)
        soften(half * 4 + 3, 1)
        weigh(15, half * 4 + 2, 0)
        weigh(15, half * 4 + 3, 1)

    def before_near_low():
        above_came(1)

        @pl.when(x == 0)
        def _():
            near_came(0)

        near_came(1)
        came(NEAR_O, 0, 1)

    def before_far_low():
        above_came(2)
        far_came(0)

        @pl.when(x != 0)
        def _():
            near_came(2)

        far_came(1)
        came(FAR_O, 0, 1)

    def before_cross():
        above_came(3)

        @pl.when(x == 0)
        def _():
            pass_relay(0, z_up)
            pass_relay(1, z_up)

        far_came(2)

        @pl.when(x != 0)
        def _():
            near_came(3)

        came(CROSS, 0, 1, 2, 3)

    def before_near_high():
        @pl.when(x == 0)
        def _():
            near_came(2)
            near_came(3)

        far_came(3)
        came(NEAR_O, 2, 3)

    def before_far_high():
        @pl.when(x == 3)
        def _():
            pass_relay(2, z_down)

        came(FAR_O, 2, 3)

    def before_mid_low():
        @pl.when(x == 3)
        def _():
            pass_relay(3, z_down)

        mid_came(0)
        mid_came(1)
        came(MID_O, 0, 1)

    def before_mid_high():
        mid_came(2)
        mid_came(3)
        came(MID_O, 2, 3)

    run_half(
        0,
        {
            0: before_near_low,
            1: before_far_low,
            2: before_cross,
            3: before_near_high,
            4: before_far_high,
            5: before_mid_low,
            6: before_mid_high,
        },
    )
    normalise(0)
    for copy in load_w:
        copy.wait()
    start_sum(0)
    own_part(0)
    start_sum(1)
    second_step(0)
    own_part(1)
    run_half(
        1,
        {1: lambda: second_step(1), 4: lambda: finish_moved(0)},
    )
    normalise(1)
    start_sum(2)
    own_part(2)
    start_sum(3)
    finish_moved(1)
    carry_moved(0)
    own_part(3)
    second_step(2)
    second_step(3)
    carry_moved(1)
    finish_kept(2)
    finish_kept(3)
    for block in (0, 1):
        copy_z(1, block).wait_recv()
        out[pl.ds((2 + block) * BLOCK, BLOCK), :] = moved_in[block]

    for q in range(4):
        for slot in (ABOVE, CROSS, NEAR, NEAR_O, FAR, FAR_O, MID_O):
            send(OWN, slot, q, sibling).wait_send()

    for q in (0, 1):
        pl.when(x != 3)(send(NEAR, MID, q, x_up).wait_send)
        pl.when(x == 3)(send_relay(NEAR, q, x_up).wait_send)
        pl.when(x == 0)(hand_over(q, z_up).wait_send)
    for q in (2, 3):
        pl.when(x != 0)(send(FAR, MID, q, x_down).wait_send)
        pl.when(x == 0)(send_relay(FAR, q, x_down).wait_send)
        pl.when(x == 3)(hand_over(q, z_down).wait_send)

    for block in range(4):
        for kind in range(3):
            for way in (0, 1):
                copy_y(kind, block, way).wait_send()
    for block in (0, 1):
        for leg in (0, 1):
            copy_z(leg, block).wait_send()


def local(queries, key_rows, value_rows, doc_lengths, block_plan, out_weight):
    tokens, width = queries.shape
    anywhere = pl.BlockSpec(memory_space=pl.ANY)
    scalars = pl.BlockSpec(memory_space=pltpu.SMEM)
    return pl.pallas_call(
        kernel,
        out_shape=jax.ShapeDtypeStruct((tokens, width), BF16),
        in_specs=[anywhere, anywhere, anywhere, scalars, scalars, anywhere],
        out_specs=pl.BlockSpec(memory_space=pltpu.VMEM),
        scratch_shapes=[
            pltpu.VMEM((4, BLOCK, width), BF16),
            pltpu.VMEM((9, T, 512), BF16),
            pltpu.VMEM((4, QUARTER, 512), BF16),
            pltpu.VMEM((4, WIDE, WIDE), BF16),
            pltpu.VMEM((16, T, 256), BF16),
            pltpu.VMEM((16, VROWS, T), BF16),
            pltpu.VMEM((8, 256, T), BF16),
            pltpu.VMEM((9, 1, T), F32),
            pltpu.VMEM((9, VROWS, T), F32),
            pltpu.VMEM((T, T), F32),
            pltpu.VMEM((T, T), F32),
            pltpu.VMEM((T, T), BF16),
            pltpu.VMEM((T, T), BF16),
            pltpu.VMEM((1, T), F32),
            pltpu.VMEM((1, T), F32),
            pltpu.VMEM((4, BLOCK, WIDE), BF16),
            pltpu.VMEM((4, 2, BLOCK, HALF), F32),
            pltpu.VMEM((3, 4, 2, BLOCK, HALF), BF16),
            pltpu.VMEM((3, 4, 2, BLOCK, HALF), BF16),
            pltpu.VMEM((2, BLOCK, WIDE), BF16),
            pltpu.VMEM((2, BLOCK, WIDE), BF16),
            pltpu.VMEM((2, BLOCK, WIDE), BF16),
            pltpu.SemaphoreType.DMA((3,)),
            pltpu.SemaphoreType.DMA((4,)),
            pltpu.SemaphoreType.DMA((11, 4)),
            pltpu.SemaphoreType.DMA((11, 4)),
            pltpu.SemaphoreType.DMA((3, 4, 2)),
            pltpu.SemaphoreType.DMA((3, 4, 2)),
            pltpu.SemaphoreType.DMA((2, 2)),
            pltpu.SemaphoreType.DMA((2, 2)),
        ],
        compiler_params=pltpu.CompilerParams(
            collective_id=0, has_side_effects=True, vmem_limit_bytes=56 << 20
        ),
        name="attend_and_project",
    )(queries.reshape(4, BLOCK, width), key_rows, value_rows, doc_lengths, block_plan, out_weight)


def solution(mesh):
    return jax.shard_map(
        local,
        mesh=mesh,
        in_specs=(
            P("seq", "head"),
            P("seq", "head"),
            P("seq", "head"),
            P(),
            P("seq"),
            P("head", None),
        ),
        out_specs=P("seq", "head"),
        check_vma=False,
    )
```

```python
import jax
import jax.numpy as jnp
from jax import lax
from jax.experimental import pallas as pl
from jax.experimental.pallas import tpu as pltpu
from jax.sharding import PartitionSpec as P

MESH = pl.DeviceIdType.MESH
F32 = jnp.float32
BF16 = jnp.bfloat16
HEAD_DIM = 128
DOCS = 64
X_CHIPS = 4
Z_CHIPS = 8
CHIPS = X_CHIPS * Z_CHIPS
HEADS = 8
KV = 2
T = 512
BLOCK = 128
WIDE = 1024
HALF = 512
VROWS = HEAD_DIM + 16
EXP_SCALE = 1.4426950408889634 / HEAD_DIM**0.5
BIG = 1e30
OWN, CROSS, NEAR, NEAR_O, FAR, FAR_O, MID, MID_O, ABOVE = range(9)
DUMMY = 8


def transposed(block):
    return block.astype(F32).T.astype(BF16)


def kernel(
    q_hbm, k_hbm, v_hbm, lens, plan, w_hbm, out,
    qv, win, relay, wbuf, ka, vat, qt, m_ref, acc, s0, s1, p0, p1, a0, a1,
    att, keep, sent, landed, res, moved_in,
    in_sem, w_sem, kv_send, kv_recv, y_send, y_recv, z_send, z_recv,
):
    index = lax.axis_index("seq")
    y = lax.axis_index("head")
    core = lax.rem(index, 2)
    chip = index // 2
    x = lax.rem(chip, X_CHIPS)
    z = chip // X_CHIPS

    def at(zz, xx, cc):
        return ((zz * X_CHIPS + xx) * 2 + cc, y)

    z_up = at(lax.rem(z + 1, Z_CHIPS), x, core)
    z_down = at(lax.rem(z + Z_CHIPS - 1, Z_CHIPS), x, core)
    x_up = at(z, lax.rem(x + 1, X_CHIPS), core)
    x_down = at(z, lax.rem(x + X_CHIPS - 1, X_CHIPS), core)
    sibling = at(z, x, 1 - core)
    partner = at(lax.rem(z + Z_CHIPS // 2, Z_CHIPS), x, core)
    y_up = (index, lax.rem(y + 1, 4))
    y_down = (index, lax.rem(y + 3, 4))

    load_k = pltpu.make_async_copy(k_hbm, win.at[OWN, :, pl.ds(0, 256)], in_sem.at[0])
    load_v = pltpu.make_async_copy(v_hbm, win.at[OWN, :, pl.ds(256, 256)], in_sem.at[1])
    load_q = pltpu.make_async_copy(q_hbm, qv, in_sem.at[2])
    load_k.start()
    load_v.start()
    load_q.start()
    load_w = []
    for step in (2, 1, 3, 0):
        group = lax.rem(y + step, 4)
        load_w.append(
            pltpu.make_async_copy(
                w_hbm.at[:, pl.ds(pl.multiple_of(group * WIDE, WIDE), WIDE)], wbuf.at[step], w_sem.at[step]
            )
        )

    barrier = pltpu.get_barrier_semaphore()
    for other in (z_up, z_down, x_up, x_down, sibling, partner, y_up, y_down):
        pl.semaphore_signal(barrier, inc=1, device_id=other, device_id_type=MESH)
    pl.semaphore_wait(barrier, 8)

    def part(ref, half):
        return ref.at[pl.ds(half * 256, 256), :]

    def send(source, slot, half, target):
        return pltpu.make_async_remote_copy(
            src_ref=part(win.at[source], half),
            dst_ref=part(win.at[slot], half),
            send_sem=kv_send.at[slot, half],
            recv_sem=kv_recv.at[slot, half],
            device_id=target,
            device_id_type=MESH,
        )

    def send_relay(source, half, way, target):
        return pltpu.make_async_remote_copy(
            src_ref=part(win.at[source], half),
            dst_ref=relay.at[way],
            send_sem=kv_send.at[9, way],
            recv_sem=kv_recv.at[9, way],
            device_id=target,
            device_id_type=MESH,
        )

    def pass_relay(half, way, target):
        return pltpu.make_async_remote_copy(
            src_ref=relay.at[way],
            dst_ref=part(win.at[MID], half),
            send_sem=kv_send.at[MID, half],
            recv_sem=kv_recv.at[MID, half],
            device_id=target,
            device_id_type=MESH,
        )

    load_k.wait()
    load_v.wait()

    for half in (0, 1):
        send(OWN, ABOVE, half, z_up).start()

        @pl.when(x < 3)
        def _():
            send(OWN, NEAR, half, x_up).start()

        @pl.when(x == 0)
        def _():
            send(OWN, FAR, half, x_down).start()

        @pl.when(core == 0)
        def _():
            send(OWN, CROSS, half, sibling).start()

    @pl.when(x == 1)
    def _():
        send_relay(OWN, 1, 1, x_down).start()

    for copy in load_w:
        copy.start()

    lane = lax.broadcasted_iota(jnp.int32, (1, HEAD_DIM), 1)
    begins = jnp.zeros((1, HEAD_DIM), jnp.int32)
    ends = jnp.zeros((1, HEAD_DIM), jnp.int32)
    for doc in range(DOCS):
        length = lens[doc]
        begins = begins + jnp.where(lane > doc, length, 0)
        ends = ends + jnp.where(lane >= doc, length, 0)
    kept0 = jnp.clip(plan[0] - index * 4, 0, 3)
    kept1 = jnp.clip(plan[1] - index * 4, 0, 3)
    moved0 = jnp.where(kept0 != 0, 0, jnp.where(kept1 != 1, 1, 2))
    moved1 = jnp.clip(6 - kept0 - kept1 - moved0, 0, 3)
    ids = (moved0, moved1, kept0, kept1)

    def same_doc(base, rows):
        pos = base + lax.broadcasted_iota(jnp.int32, (rows, HEAD_DIM), 0)
        return jnp.logical_and(pos >= begins, pos < ends)

    for g in range(KV):
        vat[g, HEAD_DIM:, :] = jnp.ones((VROWS - HEAD_DIM, 8 * T), BF16)
    s1[...] = jnp.zeros(s1.shape, F32)
    p0[...] = jnp.zeros(p0.shape, BF16)
    a0[...] = jnp.zeros(a0.shape, F32)
    load_q.wait()
    for b in range(4):
        rows = qv[ids[b]]
        marks = jnp.where(same_doc(index * T + ids[b] * BLOCK, BLOCK), 0.0, -BIG).T.astype(BF16)
        for h in range(HEADS):
            c = (b // 2) * 4 + h // 2
            col = (h % 2) * 256 + (b % 2) * BLOCK
            qt[c, :HEAD_DIM, col : col + BLOCK] = transposed(rows[:, h * HEAD_DIM : (h + 1) * HEAD_DIM])
            qt[c, HEAD_DIM:, col : col + BLOCK] = marks
    m_ref[...] = jnp.full(m_ref.shape, -3e38, F32)
    acc[...] = jnp.zeros(acc.shape, F32)

    def prepare(tile, base):
        hot = jnp.where(same_doc(base, T), 1.0, 0.0).astype(BF16)
        keys = slice(tile * T, (tile + 1) * T)
        for g in range(KV):
            ka[g, keys, :HEAD_DIM] = win[tile, :, g * HEAD_DIM : (g + 1) * HEAD_DIM]
            ka[g, keys, HEAD_DIM:] = hot
            vat[g, :HEAD_DIM, keys] = transposed(win[tile, :, 256 + g * HEAD_DIM : 256 + (g + 1) * HEAD_DIM])

    def prepare_pair(tile, distance):
        there = 2 * lax.rem(chip - distance + CHIPS, CHIPS)
        prepare(tile, (there + core) * T)
        prepare(tile + 1, (there + 1 - core) * T)

    scores, probs, scales = (s0, s1), (p0, p1), (a0, a1)

    def keys_at(start, count):
        return pl.ds(start if isinstance(start, int) else pl.multiple_of(start, 256), count)

    def score(g, start, count, c, which, causal):
        value = jnp.dot(ka[g, keys_at(start, count), :], qt[c], preferred_element_type=F32)
        if causal is not None:
            value = jnp.where(causal, value, -BIG)
        scores[which][:count] = value

    def soften(count, c, which):
        value = scores[which][:count]
        old = m_ref[c]
        new = jnp.maximum(old, jnp.max(value, axis=0, keepdims=True))
        probs[which][:count] = jnp.exp2((value - new) * EXP_SCALE).astype(BF16)
        scales[which][...] = jnp.exp2((old - new) * EXP_SCALE)
        m_ref[c] = new

    def weigh(g, start, count, c, which):
        acc[c] = acc[c] * scales[which][...] + jnp.dot(
            vat[g, :, keys_at(start, count)], probs[which][:count], preferred_element_type=F32
        )

    prepare(OWN, index * T)
    lanes = lax.broadcasted_iota(jnp.int32, (T, T), 1)
    key_row = lax.broadcasted_iota(jnp.int32, (T, T), 0)
    inner = lanes % BLOCK
    second = (lanes // BLOCK) % 2
    limits = [inner + BLOCK * jnp.where(second == 0, ids[2 * half], ids[2 * half + 1]) for half in (0, 1)]

    def own_half(half):
        causal = key_row <= limits[half]
        for u in range(4):
            score(u // 2, 0, T, half * 4 + u, u % 2, causal)
            soften(T, half * 4 + u, u % 2)
            weigh(u // 2, 0, T, half * 4 + u, u % 2)

    own_half(0)
    own_half(1)

    for half in (0, 1):
        send(OWN, ABOVE, half, z_up).wait_recv()

        @pl.when(x == 2)
        def _():
            if half == 0:
                send_relay(ABOVE, 0, 0, x_up).start()

        @pl.when(x > 0)
        def _():
            send(ABOVE, FAR, half, x_down).start()

        @pl.when(x == 3)
        def _():
            send(ABOVE, NEAR, half, x_up).start()

        @pl.when(core == 1)
        def _():
            send(ABOVE, CROSS, half, sibling).start()

    @pl.when(x == 0)
    def _():
        send_relay(OWN, 1, 1, x_down).wait_recv()
        pass_relay(1, 1, x_down).start()

    def near_came():
        for half in (0, 1):
            send(OWN, NEAR, half, x_up).wait_recv()
            send(NEAR, NEAR_O, half, sibling).start()
            if half == 0:

                @pl.when(x != 3)
                def _():
                    send(NEAR, MID, 0, x_up).start()

    @pl.when(x != 0)
    def _():
        near_came()

    def came(slot):
        for half in (0, 1):
            send(OWN, slot, half, sibling).wait_recv()

    def far_came():
        for half in (0, 1):
            send(OWN, FAR, half, x_down).wait_recv()
            send(FAR, FAR_O, half, sibling).start()
            if half == 1:

                @pl.when(x != 0)
                def _():
                    send(FAR, MID, 1, x_down).start()

    def mid_came():
        for half in (0, 1):
            send(OWN, MID, half, x_up).wait_recv()
            send(MID, MID_O, half, sibling).start()

    def copy_y(kind, block, way):
        return pltpu.make_async_remote_copy(
            src_ref=sent.at[kind, block, way],
            dst_ref=landed.at[kind, block, way],
            send_sem=y_send.at[kind, block, way],
            recv_sem=y_recv.at[kind, block, way],
            device_id=y_up if way == 0 else y_down,
            device_id_type=MESH,
        )

    def give(kind, block, way, value):
        sent[kind, block, way] = value.astype(BF16)
        copy_y(kind, block, way).start()

    def project(block, step, part_index):
        return jnp.dot(
            att[block], wbuf[step, :, part_index * HALF : (part_index + 1) * HALF], preferred_element_type=F32
        )

    def start_sum(block):
        for way in (0, 1):
            give(0, block, way, project(block, 2, way))

    def own_part(block):
        give(1, block, 0, project(block, 1, 1))
        give(1, block, 1, project(block, 3, 0))
        keep[block, 0] = project(block, 1, 0)
        keep[block, 1] = project(block, 3, 1)

    def second_step(block):
        for way in (0, 1):
            copy_y(0, block, way).wait_recv()
            give(2, block, way, keep[block, way] + landed[0, block, way].astype(F32))

    def last_step(block):
        own = [project(block, 0, 0), project(block, 0, 1)]
        for kind, way in ((1, 0), (1, 1), (2, 0), (2, 1)):
            copy_y(kind, block, way).wait_recv()
        left = own[0] + landed[2, block, 0].astype(F32) + landed[1, block, 1].astype(F32)
        right = own[1] + landed[1, block, 0].astype(F32) + landed[2, block, 1].astype(F32)
        return left.astype(BF16), right.astype(BF16)

    def copy_z(block):
        return pltpu.make_async_remote_copy(
            src_ref=res.at[block],
            dst_ref=moved_in.at[block],
            send_sem=z_send.at[block],
            recv_sem=z_recv.at[block],
            device_id=partner,
            device_id_type=MESH,
        )

    def finish_moved(block):
        left, right = last_step(block)
        res[block, :, :HALF] = left
        res[block, :, HALF:] = right
        copy_z(block).start()

    def finish_kept(block):
        left, right = last_step(block)
        out[pl.ds((block - 2) * BLOCK, BLOCK), :HALF] = left
        out[pl.ds((block - 2) * BLOCK, BLOCK), HALF:] = right

    def normalise(half):
        for u in range(4):
            c = half * 4 + u
            value = acc[c]
            rows = (value[:HEAD_DIM] / value[HEAD_DIM : HEAD_DIM + 1]).T.astype(BF16)
            for r in range(2):
                h = u * 2 + r
                for b in range(2):
                    start = r * 256 + b * BLOCK
                    att[half * 2 + b, :, h * HEAD_DIM : (h + 1) * HEAD_DIM] = rows[start : start + BLOCK]

    def run_half(half, begin, count, segments, hooks):
        def segment(s, carry):
            for when, hook in hooks.items():
                pl.when(s == when)(hook)
            first = s == 0
            start = begin + s * count
            before = jnp.where(first, start, start - count)
            for u in range(4):
                c = half * 4 + u
                score(u // 2, start, count, c, u % 2, None)
                soften(count, c - 1 if u else jnp.where(first, DUMMY, half * 4 + 3), (u + 1) % 2)
                if u >= 2:
                    weigh((u - 2) // 2, start, count, c - 2, u % 2)
                else:
                    weigh(1, before, count, jnp.where(first, DUMMY, half * 4 + 2 + u), u % 2)
            return carry

        lax.fori_loop(0, segments, segment, 0)
        last = begin + (segments - 1) * count
        soften(count, half * 4 + 3, 1)
        weigh(1, last, count, half * 4 + 2, 0)
        weigh(1, last, count, half * 4 + 3, 1)

    came(CROSS)
    prepare(CROSS, (2 * lax.rem(chip + CHIPS - jnp.where(core == 0, 4, 0), CHIPS) + 1 - core) * T)
    for u in range(4):
        score(u // 2, T, T, u, u % 2, None)
        soften(T, u, u % 2)
        weigh(u // 2, T, T, u, u % 2)

    def before_near():
        pl.when(x == 0)(near_came)
        came(NEAR_O)
        prepare_pair(NEAR, 1)

    def before_far():
        far_came()

        @pl.when(x == 3)
        def _():
            send_relay(OWN, 0, 0, x_up).wait_recv()
            pass_relay(0, 0, x_up).start()

        came(FAR_O)
        prepare_pair(FAR, 3)

    def before_mid():
        mid_came()
        came(MID_O)
        prepare_pair(MID, 2)

    run_half(0, 2 * T, 2 * T, 3, {0: before_near, 1: before_far, 2: before_mid})
    normalise(0)
    for copy in load_w:
        copy.wait()
    start_sum(0)
    own_part(0)
    start_sum(1)
    second_step(0)
    own_part(1)

    def between():
        second_step(1)
        finish_moved(0)

    run_half(1, T, 7 * T // 2, 2, {1: between})
    normalise(1)
    start_sum(2)
    own_part(2)
    start_sum(3)
    finish_moved(1)
    second_step(2)
    own_part(3)
    second_step(3)
    finish_kept(2)
    finish_kept(3)
    for block in (0, 1):
        copy_z(block).wait_recv()
        out[pl.ds((2 + block) * BLOCK, BLOCK), :] = moved_in[block]

    for half in (0, 1):
        for slot in (ABOVE, CROSS, NEAR, NEAR_O, FAR, FAR_O, MID, MID_O):
            send(OWN, slot, half, sibling).wait_send()

    @pl.when(x == 1)
    def _():
        send_relay(OWN, 1, 1, x_down).wait_send()

    @pl.when(x == 2)
    def _():
        send_relay(ABOVE, 0, 0, x_up).wait_send()

    for block in range(4):
        for kind in range(3):
            for way in (0, 1):
                copy_y(kind, block, way).wait_send()
    for block in (0, 1):
        copy_z(block).wait_send()


def local(queries, key_rows, value_rows, doc_lengths, block_plan, out_weight):
    tokens, width = queries.shape
    anywhere = pl.BlockSpec(memory_space=pl.ANY)
    scalars = pl.BlockSpec(memory_space=pltpu.SMEM)
    return pl.pallas_call(
        kernel,
        out_shape=jax.ShapeDtypeStruct((tokens, width), BF16),
        in_specs=[anywhere, anywhere, anywhere, scalars, scalars, anywhere],
        out_specs=pl.BlockSpec(memory_space=pltpu.VMEM),
        scratch_shapes=[
            pltpu.VMEM((4, BLOCK, width), BF16),
            pltpu.VMEM((9, T, 512), BF16),
            pltpu.VMEM((2, 256, 512), BF16),
            pltpu.VMEM((4, WIDE, WIDE), BF16),
            pltpu.VMEM((KV, 8 * T, 256), BF16),
            pltpu.VMEM((KV, VROWS, 8 * T), BF16),
            pltpu.VMEM((8, 256, T), BF16),
            pltpu.VMEM((9, 1, T), F32),
            pltpu.VMEM((9, VROWS, T), F32),
            pltpu.VMEM((7 * T // 2, T), F32),
            pltpu.VMEM((7 * T // 2, T), F32),
            pltpu.VMEM((7 * T // 2, T), BF16),
            pltpu.VMEM((7 * T // 2, T), BF16),
            pltpu.VMEM((1, T), F32),
            pltpu.VMEM((1, T), F32),
            pltpu.VMEM((4, BLOCK, WIDE), BF16),
            pltpu.VMEM((4, 2, BLOCK, HALF), F32),
            pltpu.VMEM((3, 4, 2, BLOCK, HALF), BF16),
            pltpu.VMEM((3, 4, 2, BLOCK, HALF), BF16),
            pltpu.VMEM((2, BLOCK, WIDE), BF16),
            pltpu.VMEM((2, BLOCK, WIDE), BF16),
            pltpu.SemaphoreType.DMA((3,)),
            pltpu.SemaphoreType.DMA((4,)),
            pltpu.SemaphoreType.DMA((10, 2)),
            pltpu.SemaphoreType.DMA((10, 2)),
            pltpu.SemaphoreType.DMA((3, 4, 2)),
            pltpu.SemaphoreType.DMA((3, 4, 2)),
            pltpu.SemaphoreType.DMA((2,)),
            pltpu.SemaphoreType.DMA((2,)),
        ],
        compiler_params=pltpu.CompilerParams(
            collective_id=0, has_side_effects=True, vmem_limit_bytes=56 << 20
        ),
        name="attend_and_project",
    )(queries.reshape(4, BLOCK, width), key_rows, value_rows, doc_lengths, block_plan, out_weight)


def solution(mesh):
    return jax.shard_map(
        local,
        mesh=mesh,
        in_specs=(
            P("seq", "head"),
            P("seq", "head"),
            P("seq", "head"),
            P(),
            P("seq"),
            P("head", None),
        ),
        out_specs=P("seq", "head"),
        check_vma=False,
    )
```

```python
import jax
import jax.numpy as jnp
from jax import lax
from jax.experimental import pallas as pl
from jax.experimental.pallas import tpu as pltpu
from jax.sharding import PartitionSpec as P

MESH = pl.DeviceIdType.MESH
F32 = jnp.float32
BF16 = jnp.bfloat16
HEAD_DIM = 128
DOCS = 64
X_CHIPS = 4
Z_CHIPS = 8
CHIPS = X_CHIPS * Z_CHIPS
HEADS = 8
KV = 2
T = 512
BLOCK = 128
QUARTER = 128
WIDE = 1024
HALF = 512
VROWS = HEAD_DIM + 16
EXP_SCALE = 1.4426950408889634 / HEAD_DIM**0.5
BIG = 1e30
OWN, CROSS, NEAR, NEAR_O, FAR, FAR_O, MID, MID_O, ABOVE = range(9)
DUMMY = 8


def transposed(block):
    return block.astype(F32).T.astype(BF16)


def kernel(
    q_hbm, k_hbm, v_hbm, lens, plan, w_hbm, out,
    qv, win, relay, wbuf, ka, vat, qt, m_ref, acc, s0, s1, p0, p1, a0, a1,
    att, keep, sent, landed, res, moved_in,
    in_sem, w_sem, kv_send, kv_recv, y_send, y_recv, z_send, z_recv,
):
    index = lax.axis_index("seq")
    y = lax.axis_index("head")
    core = lax.rem(index, 2)
    chip = index // 2
    x = lax.rem(chip, X_CHIPS)
    z = chip // X_CHIPS

    def at(zz, xx, cc):
        return ((zz * X_CHIPS + xx) * 2 + cc, y)

    z_up = at(lax.rem(z + 1, Z_CHIPS), x, core)
    z_down = at(lax.rem(z + Z_CHIPS - 1, Z_CHIPS), x, core)
    x_up = at(z, lax.rem(x + 1, X_CHIPS), core)
    x_down = at(z, lax.rem(x + X_CHIPS - 1, X_CHIPS), core)
    sibling = at(z, x, 1 - core)
    partner = at(lax.rem(z + Z_CHIPS // 2, Z_CHIPS), x, core)
    y_up = (index, lax.rem(y + 1, 4))
    y_down = (index, lax.rem(y + 3, 4))

    load_k = pltpu.make_async_copy(k_hbm, win.at[OWN, :, pl.ds(0, 256)], in_sem.at[0])
    load_v = pltpu.make_async_copy(v_hbm, win.at[OWN, :, pl.ds(256, 256)], in_sem.at[1])
    load_q = pltpu.make_async_copy(q_hbm, qv, in_sem.at[2])
    load_k.start()
    load_v.start()
    load_q.start()
    load_w = []
    for step in (2, 1, 3, 0):
        group = lax.rem(y + step, 4)
        load_w.append(
            pltpu.make_async_copy(
                w_hbm.at[:, pl.ds(pl.multiple_of(group * WIDE, WIDE), WIDE)], wbuf.at[step], w_sem.at[step]
            )
        )

    barrier = pltpu.get_barrier_semaphore()
    for other in (z_up, z_down, x_up, x_down, sibling, partner, y_up, y_down):
        pl.semaphore_signal(barrier, inc=1, device_id=other, device_id_type=MESH)
    pl.semaphore_wait(barrier, 8)

    def part(ref, q):
        return ref.at[pl.ds(q * QUARTER, QUARTER), :]

    def send(source, slot, q, target):
        return pltpu.make_async_remote_copy(
            src_ref=part(win.at[source], q),
            dst_ref=part(win.at[slot], q),
            send_sem=kv_send.at[slot, q],
            recv_sem=kv_recv.at[slot, q],
            device_id=target,
            device_id_type=MESH,
        )

    def send_relay(source, q, target):
        return pltpu.make_async_remote_copy(
            src_ref=part(win.at[source], q),
            dst_ref=relay.at[q],
            send_sem=kv_send.at[9, q],
            recv_sem=kv_recv.at[9, q],
            device_id=target,
            device_id_type=MESH,
        )

    def pass_relay(q, target):
        send_relay(OWN, q, target).wait_recv()
        pltpu.make_async_remote_copy(
            src_ref=relay.at[q],
            dst_ref=part(win.at[MID], q),
            send_sem=kv_send.at[MID, q],
            recv_sem=kv_recv.at[MID, q],
            device_id=target,
            device_id_type=MESH,
        ).start()

    load_k.wait()
    load_v.wait()

    for q in (2, 3):
        pl.when(x == 1)(send_relay(OWN, q, x_down).start)
    for q in range(4):
        send(OWN, ABOVE, q, z_up).start()
        pl.when(x < 3)(send(OWN, NEAR, q, x_up).start)
        pl.when(x == 0)(send(OWN, FAR, q, x_down).start)
        pl.when(core == 0)(send(OWN, CROSS, q, sibling).start)

    for copy in load_w:
        copy.start()

    lane = lax.broadcasted_iota(jnp.int32, (1, HEAD_DIM), 1)
    begins = jnp.zeros((1, HEAD_DIM), jnp.int32)
    ends = jnp.zeros((1, HEAD_DIM), jnp.int32)
    for doc in range(DOCS):
        length = lens[doc]
        begins = begins + jnp.where(lane > doc, length, 0)
        ends = ends + jnp.where(lane >= doc, length, 0)
    kept0 = jnp.clip(plan[0] - index * 4, 0, 3)
    kept1 = jnp.clip(plan[1] - index * 4, 0, 3)
    moved0 = jnp.where(kept0 != 0, 0, jnp.where(kept1 != 1, 1, 2))
    moved1 = jnp.clip(6 - kept0 - kept1 - moved0, 0, 3)
    ids = (moved0, moved1, kept0, kept1)

    def same_doc(base, rows):
        pos = base + lax.broadcasted_iota(jnp.int32, (rows, HEAD_DIM), 0)
        return jnp.logical_and(pos >= begins, pos < ends)

    for g in range(KV):
        vat[g, HEAD_DIM:, :] = jnp.ones((VROWS - HEAD_DIM, 8 * T), BF16)
    s1[...] = jnp.zeros(s1.shape, F32)
    p0[...] = jnp.zeros(p0.shape, BF16)
    a0[...] = jnp.zeros(a0.shape, F32)
    load_q.wait()
    for b in range(4):
        rows = qv[ids[b]]
        marks = jnp.where(same_doc(index * T + ids[b] * BLOCK, BLOCK), 0.0, -BIG).T.astype(BF16)
        for h in range(HEADS):
            c = (b // 2) * 4 + h // 2
            col = (h % 2) * 256 + (b % 2) * BLOCK
            qt[c, :HEAD_DIM, col : col + BLOCK] = transposed(rows[:, h * HEAD_DIM : (h + 1) * HEAD_DIM])
            qt[c, HEAD_DIM:, col : col + BLOCK] = marks
    m_ref[...] = jnp.full(m_ref.shape, -3e38, F32)
    acc[...] = jnp.zeros(acc.shape, F32)

    def prepare(tile, base):
        hot = jnp.where(same_doc(base, T), 1.0, 0.0).astype(BF16)
        keys = slice(tile * T, (tile + 1) * T)
        for g in range(KV):
            ka[g, keys, :HEAD_DIM] = win[tile, :, g * HEAD_DIM : (g + 1) * HEAD_DIM]
            ka[g, keys, HEAD_DIM:] = hot
            vat[g, :HEAD_DIM, keys] = transposed(win[tile, :, 256 + g * HEAD_DIM : 256 + (g + 1) * HEAD_DIM])

    def prepare_pair(tile, distance):
        there = 2 * lax.rem(chip - distance + CHIPS, CHIPS)
        prepare(tile, (there + core) * T)
        prepare(tile + 1, (there + 1 - core) * T)

    scores, probs, scales = (s0, s1), (p0, p1), (a0, a1)

    def keys_at(start, count):
        return pl.ds(start if isinstance(start, int) else pl.multiple_of(start, 256), count)

    def score(g, start, count, c, which, causal):
        value = jnp.dot(ka[g, keys_at(start, count), :], qt[c], preferred_element_type=F32)
        if causal is not None:
            value = jnp.where(causal, value, -BIG)
        scores[which][:count] = value

    def soften(count, c, which):
        value = scores[which][:count]
        old = m_ref[c]
        new = jnp.maximum(old, jnp.max(value, axis=0, keepdims=True))
        probs[which][:count] = jnp.exp2((value - new) * EXP_SCALE).astype(BF16)
        scales[which][...] = jnp.exp2((old - new) * EXP_SCALE)
        m_ref[c] = new

    def weigh(g, start, count, c, which):
        acc[c] = acc[c] * scales[which][...] + jnp.dot(
            vat[g, :, keys_at(start, count)], probs[which][:count], preferred_element_type=F32
        )

    prepare(OWN, index * T)
    lanes = lax.broadcasted_iota(jnp.int32, (1, T), 1)
    key_row = lax.broadcasted_iota(jnp.int32, (T, T), 0)
    inner = lanes % BLOCK
    second = (lanes // BLOCK) % 2
    limits = [inner + BLOCK * jnp.where(second == 0, ids[2 * half], ids[2 * half + 1]) for half in (0, 1)]

    def own_half(half):
        causal = key_row <= limits[half]
        for u in range(4):
            score(u // 2, 0, T, half * 4 + u, u % 2, causal)
            soften(T, half * 4 + u, u % 2)
            weigh(u // 2, 0, T, half * 4 + u, u % 2)

    def above_came(q):
        send(OWN, ABOVE, q, z_up).wait_recv()
        if q < 2:
            pl.when(x == 2)(send_relay(ABOVE, q, x_up).start)
        pl.when(x > 0)(send(ABOVE, FAR, q, x_down).start)
        pl.when(x == 3)(send(ABOVE, NEAR, q, x_up).start)
        pl.when(core == 1)(send(ABOVE, CROSS, q, sibling).start)

    def near_came(*quarters):
        for q in quarters:
            send(OWN, NEAR, q, x_up).wait_recv()
            if q < 2:
                pl.when(x != 3)(send(NEAR, MID, q, x_up).start)
            send(NEAR, NEAR_O, q, sibling).start()

    def far_came(q):
        send(OWN, FAR, q, x_down).wait_recv()
        if q >= 2:
            pl.when(x != 0)(send(FAR, MID, q, x_down).start)
        send(FAR, FAR_O, q, sibling).start()

    def came(slot):
        for q in range(4):
            send(OWN, slot, q, sibling).wait_recv()

    def mid_came():
        for q in range(4):
            send(OWN, MID, q, x_up).wait_recv()
            send(MID, MID_O, q, sibling).start()

    own_half(0)
    above_came(0)
    pl.when(x != 0)(lambda: near_came(0))
    own_half(1)
    above_came(1)
    pl.when(x != 0)(lambda: near_came(1))

    @pl.when(x == 0)
    def _():
        for q in (2, 3):
            pass_relay(q, x_down)

    above_came(2)
    pl.when(x != 0)(lambda: near_came(2))
    far_came(0)
    far_came(1)
    above_came(3)
    pl.when(x != 0)(lambda: near_came(3))
    pl.when(x == 0)(lambda: near_came(0, 1))

    def copy_y(kind, block, way):
        return pltpu.make_async_remote_copy(
            src_ref=sent.at[kind, block, way],
            dst_ref=landed.at[kind, block, way],
            send_sem=y_send.at[kind, block, way],
            recv_sem=y_recv.at[kind, block, way],
            device_id=y_up if way == 0 else y_down,
            device_id_type=MESH,
        )

    def give(kind, block, way, value):
        sent[kind, block, way] = value.astype(BF16)
        copy_y(kind, block, way).start()

    def project(block, step, part_index):
        return jnp.dot(
            att[block], wbuf[step, :, part_index * HALF : (part_index + 1) * HALF], preferred_element_type=F32
        )

    def start_sum(block):
        for way in (0, 1):
            give(0, block, way, project(block, 2, way))

    def own_part(block):
        give(1, block, 0, project(block, 1, 1))
        give(1, block, 1, project(block, 3, 0))
        keep[block, 0] = project(block, 1, 0)
        keep[block, 1] = project(block, 3, 1)

    def second_step(block):
        for way in (0, 1):
            copy_y(0, block, way).wait_recv()
            give(2, block, way, keep[block, way] + landed[0, block, way].astype(F32))

    def last_step(block):
        own = [project(block, 0, 0), project(block, 0, 1)]
        for kind, way in ((1, 0), (1, 1), (2, 0), (2, 1)):
            copy_y(kind, block, way).wait_recv()
        left = own[0] + landed[2, block, 0].astype(F32) + landed[1, block, 1].astype(F32)
        right = own[1] + landed[1, block, 0].astype(F32) + landed[2, block, 1].astype(F32)
        return left.astype(BF16), right.astype(BF16)

    def copy_z(block):
        return pltpu.make_async_remote_copy(
            src_ref=res.at[block],
            dst_ref=moved_in.at[block],
            send_sem=z_send.at[block],
            recv_sem=z_recv.at[block],
            device_id=partner,
            device_id_type=MESH,
        )

    def finish_moved(block):
        left, right = last_step(block)
        res[block, :, :HALF] = left
        res[block, :, HALF:] = right
        copy_z(block).start()

    def finish_kept(block):
        left, right = last_step(block)
        out[pl.ds((block - 2) * BLOCK, BLOCK), :HALF] = left
        out[pl.ds((block - 2) * BLOCK, BLOCK), HALF:] = right

    def normalise(half):
        for u in range(4):
            c = half * 4 + u
            value = acc[c]
            rows = (value[:HEAD_DIM] / value[HEAD_DIM : HEAD_DIM + 1]).T.astype(BF16)
            for r in range(2):
                h = u * 2 + r
                for b in range(2):
                    start = r * 256 + b * BLOCK
                    att[half * 2 + b, :, h * HEAD_DIM : (h + 1) * HEAD_DIM] = rows[start : start + BLOCK]

    def run_half(half, begin, count, segments, hooks):
        def segment(s, carry):
            for when, hook in hooks.items():
                pl.when(s == when)(hook)
            first = s == 0
            start = begin + s * count
            before = jnp.where(first, start, start - count)
            for u in range(4):
                c = half * 4 + u
                score(u // 2, start, count, c, u % 2, None)
                soften(count, c - 1 if u else jnp.where(first, DUMMY, half * 4 + 3), (u + 1) % 2)
                if u >= 2:
                    weigh((u - 2) // 2, start, count, c - 2, u % 2)
                else:
                    weigh(1, before, count, jnp.where(first, DUMMY, half * 4 + 2 + u), u % 2)
            return carry

        lax.fori_loop(0, segments, segment, 0)
        last = begin + (segments - 1) * count
        soften(count, half * 4 + 3, 1)
        weigh(1, last, count, half * 4 + 2, 0)
        weigh(1, last, count, half * 4 + 3, 1)

    came(CROSS)
    prepare(CROSS, (2 * lax.rem(chip + CHIPS - jnp.where(core == 0, 4, 0), CHIPS) + 1 - core) * T)
    for u in range(4):
        score(u // 2, T, T, u, u % 2, None)
        soften(T, u, u % 2)
        weigh(u // 2, T, T, u, u % 2)

    def before_near():
        far_came(2)
        pl.when(x == 0)(lambda: near_came(2, 3))
        pl.when(x == 3)(lambda: pass_relay(0, x_up))
        far_came(3)
        came(NEAR_O)
        prepare_pair(NEAR, 1)

    def before_far():
        pl.when(x == 3)(lambda: pass_relay(1, x_up))
        came(FAR_O)
        prepare_pair(FAR, 3)

    def before_mid():
        mid_came()
        came(MID_O)
        prepare_pair(MID, 2)

    run_half(0, 2 * T, 2 * T, 3, {0: before_near, 1: before_far, 2: before_mid})
    normalise(0)
    for copy in load_w:
        copy.wait()
    start_sum(0)
    own_part(0)
    start_sum(1)
    second_step(0)
    own_part(1)

    def between():
        second_step(1)
        finish_moved(0)

    run_half(1, T, 7 * T // 2, 2, {1: between})
    normalise(1)
    start_sum(2)
    own_part(2)
    start_sum(3)
    finish_moved(1)
    second_step(2)
    own_part(3)
    second_step(3)
    finish_kept(2)
    finish_kept(3)
    for block in (0, 1):
        copy_z(block).wait_recv()
        out[pl.ds((2 + block) * BLOCK, BLOCK), :] = moved_in[block]

    for q in range(4):
        for slot in (ABOVE, CROSS, NEAR, NEAR_O, FAR, FAR_O, MID, MID_O):
            send(OWN, slot, q, sibling).wait_send()
        pl.when(x == (2 if q < 2 else 1))(send_relay(OWN, q, x_up).wait_send)

    for block in range(4):
        for kind in range(3):
            for way in (0, 1):
                copy_y(kind, block, way).wait_send()
    for block in (0, 1):
        copy_z(block).wait_send()


def local(queries, key_rows, value_rows, doc_lengths, block_plan, out_weight):
    tokens, width = queries.shape
    anywhere = pl.BlockSpec(memory_space=pl.ANY)
    scalars = pl.BlockSpec(memory_space=pltpu.SMEM)
    return pl.pallas_call(
        kernel,
        out_shape=pltpu.VMEM((tokens, width), BF16),
        in_specs=[anywhere, anywhere, anywhere, scalars, scalars, anywhere],
        out_specs=pl.BlockSpec(memory_space=pltpu.VMEM),
        scratch_shapes=[
            pltpu.VMEM((4, BLOCK, width), BF16),
            pltpu.VMEM((9, T, 512), BF16),
            pltpu.VMEM((4, QUARTER, 512), BF16),
            pltpu.VMEM((4, WIDE, WIDE), BF16),
            pltpu.VMEM((KV, 8 * T, 256), BF16),
            pltpu.VMEM((KV, VROWS, 8 * T), BF16),
            pltpu.VMEM((8, 256, T), BF16),
            pltpu.VMEM((9, 1, T), F32),
            pltpu.VMEM((9, VROWS, T), F32),
            pltpu.VMEM((7 * T // 2, T), F32),
            pltpu.VMEM((7 * T // 2, T), F32),
            pltpu.VMEM((7 * T // 2, T), BF16),
            pltpu.VMEM((7 * T // 2, T), BF16),
            pltpu.VMEM((1, T), F32),
            pltpu.VMEM((1, T), F32),
            pltpu.VMEM((4, BLOCK, WIDE), BF16),
            pltpu.VMEM((4, 2, BLOCK, HALF), F32),
            pltpu.VMEM((3, 4, 2, BLOCK, HALF), BF16),
            pltpu.VMEM((3, 4, 2, BLOCK, HALF), BF16),
            pltpu.VMEM((2, BLOCK, WIDE), BF16),
            pltpu.VMEM((2, BLOCK, WIDE), BF16),
            pltpu.SemaphoreType.DMA((3,)),
            pltpu.SemaphoreType.DMA((4,)),
            pltpu.SemaphoreType.DMA((10, 4)),
            pltpu.SemaphoreType.DMA((10, 4)),
            pltpu.SemaphoreType.DMA((3, 4, 2)),
            pltpu.SemaphoreType.DMA((3, 4, 2)),
            pltpu.SemaphoreType.DMA((2,)),
            pltpu.SemaphoreType.DMA((2,)),
        ],
        compiler_params=pltpu.CompilerParams(
            collective_id=0, has_side_effects=True, vmem_limit_bytes=56 << 20
        ),
        name="attend_and_project",
    )(queries.reshape(4, BLOCK, width), key_rows, value_rows, doc_lengths, block_plan, out_weight)


def solution(mesh):
    return jax.shard_map(
        local,
        mesh=mesh,
        in_specs=(
            P("seq", "head"),
            P("seq", "head"),
            P("seq", "head"),
            P(),
            P("seq"),
            P("head", None),
        ),
        out_specs=P("seq", "head"),
        check_vma=False,
    )
```

```python
import jax
import jax.numpy as jnp
from jax import lax
from jax.experimental import pallas as pl
from jax.experimental.pallas import tpu as pltpu
from jax.sharding import PartitionSpec as P

MESH = pl.DeviceIdType.MESH
F32 = jnp.float32
BF16 = jnp.bfloat16
HEAD_DIM = 128
DOCS = 64
X_CHIPS = 4
Z_CHIPS = 8
CHIPS = X_CHIPS * Z_CHIPS
HEADS = 8
KV = 2
T = 512
BLOCK = 128
QUARTER = 128
WIDE = 1024
HALF = 512
VROWS = HEAD_DIM + 16
EXP_SCALE = 1.4426950408889634 / HEAD_DIM**0.5
BIG = 1e30
OWN, CROSS, NEAR, NEAR_O, FAR, FAR_O, MID, MID_O, ABOVE = range(9)
DUMMY = 8


def transposed(block):
    return block.astype(F32).T.astype(BF16)


def kernel(
    q_hbm, k_hbm, v_hbm, lens, plan, w_hbm, out,
    qv, win, relay, wbuf, ka, vat, qt, m_ref, acc, s0, s1, p0, p1, a0, a1,
    att, keep, sent, landed, res, moved_in,
    in_sem, w_sem, kv_send, kv_recv, y_send, y_recv, z_send, z_recv,
):
    index = lax.axis_index("seq")
    y = lax.axis_index("head")
    core = lax.rem(index, 2)
    chip = index // 2
    x = lax.rem(chip, X_CHIPS)
    z = chip // X_CHIPS

    def at(zz, xx, cc):
        return ((zz * X_CHIPS + xx) * 2 + cc, y)

    z_up = at(lax.rem(z + 1, Z_CHIPS), x, core)
    z_down = at(lax.rem(z + Z_CHIPS - 1, Z_CHIPS), x, core)
    x_up = at(z, lax.rem(x + 1, X_CHIPS), core)
    x_down = at(z, lax.rem(x + X_CHIPS - 1, X_CHIPS), core)
    sibling = at(z, x, 1 - core)
    partner = at(lax.rem(z + Z_CHIPS // 2, Z_CHIPS), x, core)
    y_up = (index, lax.rem(y + 1, 4))
    y_down = (index, lax.rem(y + 3, 4))

    load_k = pltpu.make_async_copy(k_hbm, win.at[OWN, :, pl.ds(0, 256)], in_sem.at[0])
    load_v = pltpu.make_async_copy(v_hbm, win.at[OWN, :, pl.ds(256, 256)], in_sem.at[1])
    load_q = pltpu.make_async_copy(q_hbm, qv, in_sem.at[2])
    load_k.start()
    load_v.start()
    load_q.start()
    load_w = []
    for step in (2, 1, 3, 0):
        group = lax.rem(y + step, 4)
        load_w.append(
            pltpu.make_async_copy(
                w_hbm.at[:, pl.ds(pl.multiple_of(group * WIDE, WIDE), WIDE)], wbuf.at[step], w_sem.at[step]
            )
        )

    barrier = pltpu.get_barrier_semaphore()
    for other in (z_up, z_down, x_up, x_down, sibling, partner, y_up, y_down):
        pl.semaphore_signal(barrier, inc=1, device_id=other, device_id_type=MESH)
    pl.semaphore_wait(barrier, 8)

    def part(ref, q):
        return ref.at[pl.ds(q * QUARTER, QUARTER), :]

    def send(source, slot, q, target):
        return pltpu.make_async_remote_copy(
            src_ref=part(win.at[source], q),
            dst_ref=part(win.at[slot], q),
            send_sem=kv_send.at[slot, q],
            recv_sem=kv_recv.at[slot, q],
            device_id=target,
            device_id_type=MESH,
        )

    def send_relay(source, q, target):
        return pltpu.make_async_remote_copy(
            src_ref=part(win.at[source], q),
            dst_ref=relay.at[q],
            send_sem=kv_send.at[9, q],
            recv_sem=kv_recv.at[9, q],
            device_id=target,
            device_id_type=MESH,
        )

    def pass_relay(q, target):
        send_relay(OWN, q, target).wait_recv()
        pltpu.make_async_remote_copy(
            src_ref=relay.at[q],
            dst_ref=part(win.at[MID], q),
            send_sem=kv_send.at[MID, q],
            recv_sem=kv_recv.at[MID, q],
            device_id=target,
            device_id_type=MESH,
        ).start()

    load_k.wait()
    load_v.wait()

    for q in (2, 3):
        pl.when(x == 1)(send_relay(OWN, q, x_down).start)
    for q in range(4):
        send(OWN, ABOVE, q, z_up).start()
        pl.when(x < 3)(send(OWN, NEAR, q, x_up).start)
        pl.when(x == 0)(send(OWN, FAR, q, x_down).start)
        pl.when(core == 0)(send(OWN, CROSS, q, sibling).start)

    for copy in load_w:
        copy.start()

    lane = lax.broadcasted_iota(jnp.int32, (1, HEAD_DIM), 1)
    begins = jnp.zeros((1, HEAD_DIM), jnp.int32)
    ends = jnp.zeros((1, HEAD_DIM), jnp.int32)
    for doc in range(DOCS):
        length = lens[doc]
        begins = begins + jnp.where(lane > doc, length, 0)
        ends = ends + jnp.where(lane >= doc, length, 0)
    kept0 = jnp.clip(plan[0] - index * 4, 0, 3)
    kept1 = jnp.clip(plan[1] - index * 4, 0, 3)
    moved0 = jnp.where(kept0 != 0, 0, jnp.where(kept1 != 1, 1, 2))
    moved1 = jnp.clip(6 - kept0 - kept1 - moved0, 0, 3)
    ids = (moved0, moved1, kept0, kept1)

    def same_doc(base, rows):
        pos = base + lax.broadcasted_iota(jnp.int32, (rows, HEAD_DIM), 0)
        return jnp.logical_and(pos >= begins, pos < ends)

    for g in range(KV):
        vat[g, HEAD_DIM:, :] = jnp.ones((VROWS - HEAD_DIM, 8 * T), BF16)
    s1[...] = jnp.zeros(s1.shape, F32)
    p0[...] = jnp.zeros(p0.shape, BF16)
    a0[...] = jnp.zeros(a0.shape, F32)
    load_q.wait()
    for b in range(4):
        rows = qv[ids[b]]
        marks = jnp.where(same_doc(index * T + ids[b] * BLOCK, BLOCK), 0.0, -BIG).T.astype(BF16)
        for h in range(HEADS):
            c = (b // 2) * 4 + h // 2
            col = (h % 2) * 256 + (b % 2) * BLOCK
            qt[c, :HEAD_DIM, col : col + BLOCK] = transposed(rows[:, h * HEAD_DIM : (h + 1) * HEAD_DIM])
            qt[c, HEAD_DIM:, col : col + BLOCK] = marks
    m_ref[...] = jnp.full(m_ref.shape, -3e38, F32)
    acc[...] = jnp.zeros(acc.shape, F32)

    def prepare(tile, base):
        hot = jnp.where(same_doc(base, T), 1.0, 0.0).astype(BF16)
        keys = slice(tile * T, (tile + 1) * T)
        for g in range(KV):
            ka[g, keys, :HEAD_DIM] = win[tile, :, g * HEAD_DIM : (g + 1) * HEAD_DIM]
            ka[g, keys, HEAD_DIM:] = hot
            vat[g, :HEAD_DIM, keys] = transposed(win[tile, :, 256 + g * HEAD_DIM : 256 + (g + 1) * HEAD_DIM])

    def prepare_pair(tile, distance):
        there = 2 * lax.rem(chip - distance + CHIPS, CHIPS)
        prepare(tile, (there + core) * T)
        prepare(tile + 1, (there + 1 - core) * T)

    scores, probs, scales = (s0, s1), (p0, p1), (a0, a1)

    def keys_at(start, count):
        return pl.ds(start if isinstance(start, int) else pl.multiple_of(start, 256), count)

    def score(g, start, count, c, which, causal):
        value = jnp.dot(ka[g, keys_at(start, count), :], qt[c], preferred_element_type=F32)
        if causal is not None:
            value = jnp.where(causal, value, -BIG)
        scores[which][:count] = value

    def soften(count, c, which):
        value = scores[which][:count]
        old = m_ref[c]
        new = jnp.maximum(old, jnp.max(value, axis=0, keepdims=True))
        probs[which][:count] = jnp.exp2((value - new) * EXP_SCALE).astype(BF16)
        scales[which][...] = jnp.exp2((old - new) * EXP_SCALE)
        m_ref[c] = new

    def weigh(g, start, count, c, which):
        acc[c] = acc[c] * scales[which][...] + jnp.dot(
            vat[g, :, keys_at(start, count)], probs[which][:count], preferred_element_type=F32
        )

    prepare(OWN, index * T)
    lanes = lax.broadcasted_iota(jnp.int32, (1, T), 1)
    key_row = lax.broadcasted_iota(jnp.int32, (T, T), 0)
    inner = lanes % BLOCK
    second = (lanes // BLOCK) % 2
    limits = [inner + BLOCK * jnp.where(second == 0, ids[2 * half], ids[2 * half + 1]) for half in (0, 1)]

    def own_half(half):
        causal = key_row <= limits[half]
        for u in range(4):
            score(u // 2, 0, T, half * 4 + u, u % 2, causal)
            soften(T, half * 4 + u, u % 2)
            weigh(u // 2, 0, T, half * 4 + u, u % 2)

    def above_came(q):
        send(OWN, ABOVE, q, z_up).wait_recv()
        if q < 2:
            pl.when(x == 2)(send_relay(ABOVE, q, x_up).start)
        pl.when(x > 0)(send(ABOVE, FAR, q, x_down).start)
        pl.when(x == 3)(send(ABOVE, NEAR, q, x_up).start)
        pl.when(core == 1)(send(ABOVE, CROSS, q, sibling).start)

    def near_came(*quarters):
        for q in quarters:
            send(OWN, NEAR, q, x_up).wait_recv()
            if q < 2:
                pl.when(x != 3)(send(NEAR, MID, q, x_up).start)
            send(NEAR, NEAR_O, q, sibling).start()

    def far_came(q):
        send(OWN, FAR, q, x_down).wait_recv()
        if q >= 2:
            pl.when(x != 0)(send(FAR, MID, q, x_down).start)
        send(FAR, FAR_O, q, sibling).start()

    def came(slot):
        for q in range(4):
            send(OWN, slot, q, sibling).wait_recv()

    def mid_came(q):
        send(OWN, MID, q, x_up).wait_recv()
        send(MID, MID_O, q, sibling).start()

    own_half(0)
    above_came(0)
    pl.when(x != 0)(lambda: near_came(0))
    own_half(1)
    above_came(1)
    pl.when(x != 0)(lambda: near_came(1))

    @pl.when(x == 0)
    def _():
        for q in (2, 3):
            pass_relay(q, x_down)

    above_came(2)
    pl.when(x != 0)(lambda: near_came(2))
    far_came(0)
    far_came(1)
    above_came(3)
    pl.when(x != 0)(lambda: near_came(3))
    pl.when(x == 0)(lambda: near_came(0, 1))

    def copy_y(kind, block, way):
        return pltpu.make_async_remote_copy(
            src_ref=sent.at[kind, block, way],
            dst_ref=landed.at[kind, block, way],
            send_sem=y_send.at[kind, block, way],
            recv_sem=y_recv.at[kind, block, way],
            device_id=y_up if way == 0 else y_down,
            device_id_type=MESH,
        )

    def give(kind, block, way, value):
        sent[kind, block, way] = value.astype(BF16)
        copy_y(kind, block, way).start()

    def project(block, step, part_index):
        return jnp.dot(
            att[block], wbuf[step, :, part_index * HALF : (part_index + 1) * HALF], preferred_element_type=F32
        )

    def start_sum(block):
        for way in (0, 1):
            give(0, block, way, project(block, 2, way))

    def own_part(block):
        give(1, block, 0, project(block, 1, 1))
        give(1, block, 1, project(block, 3, 0))
        keep[block, 0] = project(block, 1, 0)
        keep[block, 1] = project(block, 3, 1)

    def second_step(block):
        for way in (0, 1):
            copy_y(0, block, way).wait_recv()
            give(2, block, way, keep[block, way] + landed[0, block, way].astype(F32))

    def last_step(block):
        own = [project(block, 0, 0), project(block, 0, 1)]
        for kind, way in ((1, 0), (1, 1), (2, 0), (2, 1)):
            copy_y(kind, block, way).wait_recv()
        left = own[0] + landed[2, block, 0].astype(F32) + landed[1, block, 1].astype(F32)
        right = own[1] + landed[1, block, 0].astype(F32) + landed[2, block, 1].astype(F32)
        return left.astype(BF16), right.astype(BF16)

    def copy_z(block):
        return pltpu.make_async_remote_copy(
            src_ref=res.at[block],
            dst_ref=moved_in.at[block],
            send_sem=z_send.at[block],
            recv_sem=z_recv.at[block],
            device_id=partner,
            device_id_type=MESH,
        )

    def finish_moved(block):
        left, right = last_step(block)
        res[block, :, :HALF] = left
        res[block, :, HALF:] = right
        copy_z(block).start()

    def finish_kept(block):
        left, right = last_step(block)
        out[pl.ds((block - 2) * BLOCK, BLOCK), :HALF] = left
        out[pl.ds((block - 2) * BLOCK, BLOCK), HALF:] = right

    def normalise(half):
        for u in range(4):
            c = half * 4 + u
            value = acc[c]
            rows = (value[:HEAD_DIM] / value[HEAD_DIM : HEAD_DIM + 1]).T.astype(BF16)
            for r in range(2):
                h = u * 2 + r
                for b in range(2):
                    start = r * 256 + b * BLOCK
                    att[half * 2 + b, :, h * HEAD_DIM : (h + 1) * HEAD_DIM] = rows[start : start + BLOCK]

    def run_half(half, begin, count, segments, hooks):
        def segment(s, carry):
            for when, hook in hooks.items():
                pl.when(s == when)(hook)
            first = s == 0
            start = begin + s * count
            before = jnp.where(first, start, start - count)
            for u in range(4):
                c = half * 4 + u
                score(u // 2, start, count, c, u % 2, None)
                soften(count, c - 1 if u else jnp.where(first, DUMMY, half * 4 + 3), (u + 1) % 2)
                if u >= 2:
                    weigh((u - 2) // 2, start, count, c - 2, u % 2)
                else:
                    weigh(1, before, count, jnp.where(first, DUMMY, half * 4 + 2 + u), u % 2)
            return carry

        lax.fori_loop(0, segments, segment, 0)
        last = begin + (segments - 1) * count
        soften(count, half * 4 + 3, 1)
        weigh(1, last, count, half * 4 + 2, 0)
        weigh(1, last, count, half * 4 + 3, 1)

    came(CROSS)
    prepare(CROSS, (2 * lax.rem(chip + CHIPS - jnp.where(core == 0, 4, 0), CHIPS) + 1 - core) * T)
    for u in range(4):
        score(u // 2, T, T, u, u % 2, None)
        soften(T, u, u % 2)
        weigh(u // 2, T, T, u, u % 2)

    def before_near():
        far_came(2)
        pl.when(x == 0)(lambda: near_came(2, 3))
        pl.when(x == 3)(lambda: pass_relay(0, x_up))
        far_came(3)
        came(NEAR_O)
        prepare_pair(NEAR, 1)

    def before_far():
        pl.when(x == 3)(lambda: pass_relay(1, x_up))
        came(FAR_O)
        prepare_pair(FAR, 3)

    def before_mid(high):
        for q in (2 * high, 2 * high + 1):
            mid_came(q)
        there = 2 * lax.rem(chip - 2 + CHIPS, CHIPS)
        rows = slice(high * 256, high * 256 + 256)
        for spot, (slot, side) in enumerate(((MID, core), (MID_O, 1 - core))):
            if spot == 1:
                for q in (2 * high, 2 * high + 1):
                    send(OWN, MID_O, q, sibling).wait_recv()
            first_key = MID * T + high * T + spot * 256
            keys = slice(first_key, first_key + 256)
            hot = jnp.where(same_doc((there + side) * T + high * 256, 256), 1.0, 0.0).astype(BF16)
            for g in range(KV):
                ka[g, keys, :HEAD_DIM] = win[slot, rows, g * HEAD_DIM : (g + 1) * HEAD_DIM]
                ka[g, keys, HEAD_DIM:] = hot
                vat[g, :HEAD_DIM, keys] = transposed(
                    win[slot, rows, 256 + g * HEAD_DIM : 256 + (g + 1) * HEAD_DIM]
                )

    run_half(0, 2 * T, 2 * T, 2, {0: before_near, 1: before_far})
    run_half(0, MID * T, T, 2, {0: lambda: before_mid(0), 1: lambda: before_mid(1)})
    normalise(0)
    for copy in load_w:
        copy.wait()
    start_sum(0)
    own_part(0)
    start_sum(1)
    second_step(0)
    own_part(1)

    def between():
        second_step(1)
        finish_moved(0)

    run_half(1, T, 7 * T // 2, 2, {1: between})
    normalise(1)
    start_sum(2)
    own_part(2)
    start_sum(3)
    finish_moved(1)
    second_step(2)
    own_part(3)
    second_step(3)
    finish_kept(2)
    finish_kept(3)
    for block in (0, 1):
        copy_z(block).wait_recv()
        out[pl.ds((2 + block) * BLOCK, BLOCK), :] = moved_in[block]

    for q in range(4):
        for slot in (ABOVE, CROSS, NEAR, NEAR_O, FAR, FAR_O, MID, MID_O):
            send(OWN, slot, q, sibling).wait_send()
        pl.when(x == (2 if q < 2 else 1))(send_relay(OWN, q, x_up).wait_send)

    for block in range(4):
        for kind in range(3):
            for way in (0, 1):
                copy_y(kind, block, way).wait_send()
    for block in (0, 1):
        copy_z(block).wait_send()


def local(queries, key_rows, value_rows, doc_lengths, block_plan, out_weight):
    tokens, width = queries.shape
    anywhere = pl.BlockSpec(memory_space=pl.ANY)
    scalars = pl.BlockSpec(memory_space=pltpu.SMEM)
    return pl.pallas_call(
        kernel,
        out_shape=pltpu.VMEM((tokens, width), BF16),
        in_specs=[anywhere, anywhere, anywhere, scalars, scalars, anywhere],
        out_specs=pl.BlockSpec(memory_space=pltpu.VMEM),
        scratch_shapes=[
            pltpu.VMEM((4, BLOCK, width), BF16),
            pltpu.VMEM((9, T, 512), BF16),
            pltpu.VMEM((4, QUARTER, 512), BF16),
            pltpu.VMEM((4, WIDE, WIDE), BF16),
            pltpu.VMEM((KV, 8 * T, 256), BF16),
            pltpu.VMEM((KV, VROWS, 8 * T), BF16),
            pltpu.VMEM((8, 256, T), BF16),
            pltpu.VMEM((9, 1, T), F32),
            pltpu.VMEM((9, VROWS, T), F32),
            pltpu.VMEM((7 * T // 2, T), F32),
            pltpu.VMEM((7 * T // 2, T), F32),
            pltpu.VMEM((7 * T // 2, T), BF16),
            pltpu.VMEM((7 * T // 2, T), BF16),
            pltpu.VMEM((1, T), F32),
            pltpu.VMEM((1, T), F32),
            pltpu.VMEM((4, BLOCK, WIDE), BF16),
            pltpu.VMEM((4, 2, BLOCK, HALF), F32),
            pltpu.VMEM((3, 4, 2, BLOCK, HALF), BF16),
            pltpu.VMEM((3, 4, 2, BLOCK, HALF), BF16),
            pltpu.VMEM((2, BLOCK, WIDE), BF16),
            pltpu.VMEM((2, BLOCK, WIDE), BF16),
            pltpu.SemaphoreType.DMA((3,)),
            pltpu.SemaphoreType.DMA((4,)),
            pltpu.SemaphoreType.DMA((10, 4)),
            pltpu.SemaphoreType.DMA((10, 4)),
            pltpu.SemaphoreType.DMA((3, 4, 2)),
            pltpu.SemaphoreType.DMA((3, 4, 2)),
            pltpu.SemaphoreType.DMA((2,)),
            pltpu.SemaphoreType.DMA((2,)),
        ],
        compiler_params=pltpu.CompilerParams(
            collective_id=0, has_side_effects=True, vmem_limit_bytes=56 << 20
        ),
        name="attend_and_project",
    )(queries.reshape(4, BLOCK, width), key_rows, value_rows, doc_lengths, block_plan, out_weight)


def solution(mesh):
    return jax.shard_map(
        local,
        mesh=mesh,
        in_specs=(
            P("seq", "head"),
            P("seq", "head"),
            P("seq", "head"),
            P(),
            P("seq"),
            P("head", None),
        ),
        out_specs=P("seq", "head"),
        check_vma=False,
    )
```
